128 devices in a mesh: row: 16 (over y, x), col: 8 (over z, core).
Axes of the slice: x: 4, y: 4, z: 4, core: 2. Of those that a mesh axis runs over, the one named last changes fastest.
Arguments:
- single: bfloat16 [6144, 768], P('row'), may hold values from -6 to 6
- pair_bias: bfloat16 [16, 6144, 6144], P(None, 'row', 'col'), may hold values from -8 to 304, as said below
- key_live: int32 [6144], P('col'), may hold values 0 or 1
- w_query: bfloat16 [768, 768], replicated, may hold values from -0.21875 to 0.21875
- w_key: bfloat16 [768, 768], replicated, may hold values from -0.21875 to 0.21875
- w_value: bfloat16 [768, 768], replicated, may hold values from -0.21875 to 0.21875
- w_gate: bfloat16 [768, 768], replicated, may hold values from -0.21875 to 0.21875
- w_out: bfloat16 [768, 768], replicated, may hold values from -0.21875 to 0.21875
- cotangent: bfloat16 [6144, 768], P('row'), may hold values from -6 to 6
Outputs:
- attended: bfloat16 [6144, 768], P('row')
- d_bias: bfloat16 [16, 6144, 6144], P(None, 'row', 'col')
- d_single: bfloat16 [6144, 768], P('row')
The draws below stay inside these ranges and needn't reach their ends.
Inputs may be any that keep to these rules, and one draw needn't show every extreme that they name: `pair_bias`: per-head additive scores.
All inputs are finite; a program needn't handle non-finite values. No bound on the sum of `key_live` on one device may be relied on, other than what follows from the above.
Results may differ from the reference program's by a relative error of at most 0.034.
Values may be sent and summed in bfloat16 or wider, within the bound.
No kernel may reach another device: no remote copies, remote signals or barrier semaphores. Data moves between devices by JAX's collectives and lax.ppermute only.
A program may use at most 128 MiB of HBM per device.

```python
import math
import jax
import jax.numpy as jnp
from jax import lax

D = 768
HEADS = 16
HD = 48
TOKENS = 6144


def draw_pair_bias(key, part):
    key = jax.random.fold_in(key, 11)
    keys = jax.random.split(key, 1)
    shape = (HEADS, TOKENS, TOKENS)
    return jax.random.uniform(keys[0], shape, jnp.float32, -8.0, -7.0).astype(jnp.bfloat16)


def set_ends(result, stream_key, smallest, top_value):
    longest = result.shape.index(max(result.shape))
    spots = []
    for shift in (0, 1):
        where = [jax.random.randint(jax.random.fold_in(stream_key, axis), (), 0, length) for axis, length in enumerate(result.shape)]
        where[longest] = (where[longest] + shift) % result.shape[longest]
        spots.append(tuple(where))
    return result.at[spots[0]].set(smallest).at[spots[1]].set(top_value)


def shard_levels(key, shape, cuts, smallest, largest):
    gain = 1.0
    for dim, blocks in cuts:
        steps = jax.random.uniform(jax.random.fold_in(jax.random.fold_in(key, 6), dim), (blocks,), jnp.float32, smallest / len(cuts), largest / len(cuts))
        gain = gain * jnp.repeat(jnp.exp(steps), shape[dim] // blocks).reshape((-1,) + (1,) * (len(shape) - 1 - dim))
    return gain


def noise(stream_key, shape, deviation, bound, cuts=(), held_as=jnp.bfloat16):
    drawn = deviation * jax.random.normal(stream_key, shape, jnp.float32)
    if cuts:
        drawn = drawn * shard_levels(stream_key, shape, cuts, -0.22, 0.18)
    return jnp.clip(drawn, -bound, bound).astype(held_as)


def setup_inputs(seed: int = 0) -> dict:
    splits = jax.random.split(jax.random.key(seed), 10)
    return {
        "single": noise(splits[0], (TOKENS, D), 1.0, 6.0, ((0, 16),)),
        "pair_bias": draw_pair_bias(jax.random.fold_in(splits[9], 71), 0),
        "key_live": set_ends((jax.random.randint(splits[2], (TOKENS,), 0, 4) < 3).astype(jnp.int32), jax.random.fold_in(splits[2], 1), 0, 1),
        "w_query": noise(splits[3], (D, D), D ** -0.5, 0.21875),
        "w_key": noise(splits[4], (D, D), D ** -0.5, 0.21875),
        "w_value": noise(splits[5], (D, D), D ** -0.5, 0.21875),
        "w_gate": noise(splits[6], (D, D), D ** -0.5, 0.21875),
        "w_out": noise(splits[7], (D, D), D ** -0.5, 0.21875),
        "cotangent": noise(splits[8], (TOKENS, D), 1.0, 6.0, ((0, 16),)),
    }


def dot_t(left, right):
    return lax.dot_general(left, right, (((1,), (1,)), ((), ())), preferred_element_type=jnp.float32)

def reference(single, pair_bias, key_live, w_query, w_key, w_value, w_gate, w_out, cotangent):
    scale = 1.0 / math.sqrt(HD)
    query = jnp.dot(single, w_query, preferred_element_type=jnp.float32).astype(jnp.bfloat16)
    keys = jnp.dot(single, w_key, preferred_element_type=jnp.float32).astype(jnp.bfloat16)
    values = jnp.dot(single, w_value, preferred_element_type=jnp.float32).astype(jnp.bfloat16)
    gate = jax.nn.sigmoid(jnp.dot(single, w_gate, preferred_element_type=jnp.float32))
    live = (key_live > 0)[None, :]
    q_heads = query.reshape(TOKENS, HEADS, HD).transpose(1, 0, 2)
    k_heads = keys.reshape(TOKENS, HEADS, HD).transpose(1, 0, 2)
    v_heads = values.reshape(TOKENS, HEADS, HD).transpose(1, 0, 2)

    def scores_of(q_one, k_one, b_one):
        raw = jnp.dot(q_one, k_one.T, preferred_element_type=jnp.float32) * scale + b_one.astype(jnp.float32)
        return jnp.where(live, raw, -30000.0)

    def forward(pieces):
        q_one, k_one, v_one, b_one = pieces
        scores = scores_of(q_one, k_one, b_one)
        top = lax.optimization_barrier(jnp.max(scores, axis=-1, keepdims=True))
        expo = jnp.exp(scores - top)
        total = lax.optimization_barrier(jnp.sum(expo, axis=-1, keepdims=True))
        out = jnp.dot(expo.astype(jnp.bfloat16), v_one, preferred_element_type=jnp.float32) / total
        return (out, top, total)
    heads_out, tops, totals = lax.map(forward, (q_heads, k_heads, v_heads, pair_bias))
    heads_cat = heads_out.transpose(1, 0, 2).reshape(TOKENS, D)
    hidden = (heads_cat * gate).astype(jnp.bfloat16)
    attended = jnp.dot(hidden, w_out, preferred_element_type=jnp.float32).astype(jnp.bfloat16)
    d_hidden = dot_t(cotangent, w_out)
    d_heads = d_hidden * gate
    d_gate = (d_hidden * heads_cat * gate * (1.0 - gate)).astype(jnp.bfloat16)
    delta = lax.optimization_barrier(jnp.sum((d_heads * heads_cat).reshape(TOKENS, HEADS, HD), axis=-1)).T
    d_heads_b = d_heads.astype(jnp.bfloat16).reshape(TOKENS, HEADS, HD).transpose(1, 0, 2)

    def backward(pieces):
        q_one, k_one, v_one, b_one, top, total, dl, dh = pieces
        prob = jnp.exp(scores_of(q_one, k_one, b_one) - top) / total
        d_val = jnp.dot(prob.astype(jnp.bfloat16).T, dh, preferred_element_type=jnp.float32)
        d_prob = jnp.dot(dh, v_one.T, preferred_element_type=jnp.float32)
        d_score = (prob * (d_prob - dl[:, None])).astype(jnp.bfloat16)
        d_q = jnp.dot(d_score, k_one, preferred_element_type=jnp.float32) * scale
        d_k = jnp.dot(d_score.T, q_one, preferred_element_type=jnp.float32) * scale
        return (d_score, d_q, d_k, d_val)
    d_bias, d_q, d_k, d_v = lax.map(backward, (q_heads, k_heads, v_heads, pair_bias, tops, totals, delta, d_heads_b))

    def merge_heads(grad):
        return grad.transpose(1, 0, 2).reshape(TOKENS, D).astype(jnp.bfloat16)
    d_single = dot_t(merge_heads(d_q), w_query) + dot_t(merge_heads(d_k), w_key)
    d_single = d_single + dot_t(merge_heads(d_v), w_value) + dot_t(d_gate, w_gate)
    return (attended, d_bias, d_single.astype(jnp.bfloat16))
```

```python
import functools
import math

import jax
import jax.numpy as jnp
from jax import lax
from jax.experimental import pallas as pl
from jax.experimental.pallas import tpu as pltpu
from jax.sharding import PartitionSpec as P

HEADS = 16
HD = 48
SLOT = 64
PAIRS = HEADS // 2
WIDE = HEADS * SLOT
LOG2E = math.log2(math.e)
LN2 = math.log(2.0)
ROWS, COLS, SIDE = 16, 8, 4
VMEM = 56 * 1024 * 1024
F32, BF16 = jnp.float32, jnp.bfloat16


def nt(left, right):
    return lax.dot_general(left, right, (((1,), (1,)), ((), ())), preferred_element_type=F32)


def nn(left, right):
    return jnp.dot(left, right, preferred_element_type=F32)


def tn(left, right):
    return lax.dot_general(left, right, (((0,), (0,)), ((), ())), preferred_element_type=F32)


def lane_of(shape):
    return lax.broadcasted_iota(jnp.int32, shape, len(shape) - 1)


def along_x(k):
    return [(y * SIDE + x, y * SIDE + (x + k) % SIDE) for y in range(SIDE) for x in range(SIDE)]


def along_y(k):
    return [(y * SIDE + x, (y + k) % SIDE * SIDE + x) for y in range(SIDE) for x in range(SIDE)]


def along_col(k):
    return [(c, (c + k) % COLS) for c in range(COLS)]


def home_to_block():
    half = ROWS // 2
    return [
        (row * COLS + col, ((row % 2) * half + col) * COLS + row // 2)
        for row in range(ROWS)
        for col in range(COLS)
    ]


def params(**more):
    return pltpu.CompilerParams(vmem_limit_bytes=VMEM, **more)


def whole(count):
    return [pl.BlockSpec(memory_space=pltpu.VMEM)] * count


SCALAR = pl.BlockSpec(memory_space=pltpu.SMEM)


def place_kernel(at_ref, *refs):
    *pieces, out = refs
    size = pieces[0].shape[0]
    for k, piece in enumerate(pieces):
        out[pl.ds(pl.multiple_of(at_ref[k], size), size), :] = piece[...]


def place(pieces, at):
    rows = sum(p.shape[0] for p in pieces)
    return pl.pallas_call(
        place_kernel,
        out_shape=jax.ShapeDtypeStruct((rows, pieces[0].shape[1]), pieces[0].dtype),
        in_specs=[SCALAR] + whole(len(pieces)),
        out_specs=pl.BlockSpec(memory_space=pltpu.VMEM),
        compiler_params=params(),
    )(at, *pieces)


def project_kernel(at_ref, *refs):
    *pieces, wk_ref, wv_ref, k_ref, v_ref = refs
    size = pieces[0].shape[0]
    spare = lane_of((size, WIDE)) % SLOT >= HD
    for n, piece in enumerate(pieces):
        rows = pl.ds(pl.multiple_of(at_ref[n], size), size)
        k_ref[rows, :] = nn(piece[...], wk_ref[...]).astype(BF16)
        v_ref[rows, :] = jnp.where(spare, 1.0, nn(piece[...], wv_ref[...])).astype(BF16)


def project(pieces, at, wk, wv):
    span = sum(p.shape[0] for p in pieces)
    shape = jax.ShapeDtypeStruct((span, WIDE), BF16)
    return pl.pallas_call(
        project_kernel,
        out_shape=(shape, shape),
        in_specs=[SCALAR] + whole(len(pieces) + 2),
        out_specs=tuple(whole(2)),
        compiler_params=params(),
    )(at, *pieces, wk, wv)


def forward_kernel(bias_ref, q_ref, k_ref, v_ref, live_ref, dead_ref, row_ref, dh_ref, expo_ref, acc_ref, stats_ref):
    pair = pl.program_id(0)
    rows = q_ref.shape[0]
    lane = lane_of((rows, 2 * SLOT))
    keys = k_ref[...] * live_ref[...] + dead_ref[...]
    values = v_ref[...]
    halves = []
    for i in range(2):
        mine = lane // SLOT == i
        query = jnp.where(mine, q_ref[...], 0)
        scores = nt(query, keys) + bias_ref[i].astype(F32) * row_ref[0:1, :]
        top = jnp.max(scores, axis=-1, keepdims=True)
        expo = jnp.exp2(scores - top).astype(BF16)
        expo_ref[i] = expo
        out = nn(expo, values)
        inner = jnp.where(mine & (lane % SLOT < HD), out * dh_ref[...], 0.0)
        inner = jnp.sum(inner, axis=-1, keepdims=True)
        out = jnp.where(lane % SLOT == HD + 1, top, out)
        halves.append(jnp.where(lane % SLOT == HD + 2, inner, out))
    acc = jnp.where(lane < SLOT, halves[0], halves[1])
    acc_ref[...] = acc
    turned = acc.T
    for i in range(2):
        for stat in range(3):
            spot = i * SLOT + HD + stat
            stats_ref[pl.ds(stat * HEADS + 2 * pair + i, 1), :] = turned[spot : spot + 1, :]


def forward(bias, q, k, v, live, dead, row, dh):
    rows, span = bias.shape[1:]
    wide = lambda n: pl.BlockSpec((n, 2 * SLOT), lambda p: (0, p))
    still = lambda *s: pl.BlockSpec(s, lambda p: (0,) * len(s))
    tile = pl.BlockSpec((2, rows, span), lambda p: (p, 0, 0))
    return pl.pallas_call(
        forward_kernel,
        grid=(PAIRS,),
        out_shape=(
            jax.ShapeDtypeStruct((HEADS, rows, span), BF16),
            jax.ShapeDtypeStruct((rows, WIDE), F32),
            jax.ShapeDtypeStruct((3 * HEADS, rows), F32),
        ),
        in_specs=[tile, wide(rows), wide(span), wide(span), still(span, 2 * SLOT), still(span, 2 * SLOT), still(8, span), wide(rows)],
        out_specs=(tile, wide(rows), still(3 * HEADS, rows)),
        compiler_params=params(),
        cost_estimate=pl.CostEstimate(flops=4 * HEADS * rows * span * 256, bytes_accessed=4 * HEADS * rows * span, transcendentals=HEADS * rows * span),
    )(bias, q, k, v, live, dead, row, dh)


def combine_kernel(at_ref, *refs):
    stats, (acc_ref, dh_ref, dhf_ref), pieces = refs[:COLS], refs[COLS : COLS + 3], refs[COLS + 3 : -1]
    own_ref = refs[-1]
    rows = acc_ref.shape[0]
    tops = [s[HEADS : 2 * HEADS, :] for s in stats]
    top = functools.reduce(jnp.maximum, tops)
    total = jnp.zeros_like(top)
    inner = jnp.zeros_like(top)
    for s, t in zip(stats, tops):
        weight = jnp.exp2(t - top)
        total += weight * s[:HEADS, :]
        inner += weight * s[2 * HEADS :, :]
    factor = jnp.exp2(tops[0] - top) / total
    shift = -factor * (inner / total)
    both = jnp.concatenate([factor, shift, jnp.zeros((128 - 2 * HEADS, rows), F32)], axis=0).T
    source = lax.broadcasted_iota(jnp.int32, (128, WIDE), 0)
    lane = lane_of((128, WIDE))
    head, spot = lane // SLOT, lane % SLOT
    spread = jnp.zeros((rows, WIDE), F32)
    for part in range(3):
        rounded = both.astype(BF16)
        both = both - rounded.astype(F32)
        pick = (source == head) & (spot < HD) | (source == head + HEADS) & (spot == HD + part)
        spread += nn(rounded, pick.astype(BF16))
    dhf_ref[...] = (spread * dh_ref[...]).astype(BF16)
    own_ref[...] = jnp.where(lane_of((rows, WIDE)) % SLOT < HD, acc_ref[...] * spread, 0.0)
    size = rows // COLS
    for k, piece in enumerate(pieces):
        piece[...] = own_ref[pl.ds(pl.multiple_of(at_ref[k], size), size), :].astype(BF16)


def combine(at, stats, acc, dh):
    rows = acc.shape[0]
    return pl.pallas_call(
        combine_kernel,
        out_shape=[jax.ShapeDtypeStruct((rows, WIDE), BF16)] + [jax.ShapeDtypeStruct((rows // COLS, WIDE), BF16)] * COLS,
        in_specs=[SCALAR] + whole(COLS + 2),
        out_specs=whole(COLS + 1),
        scratch_shapes=[pltpu.VMEM((rows, WIDE), F32)],
        compiler_params=params(),
    )(at, *stats, acc, dh)


def backward_kernel(yat_ref, cat_ref, expo_ref, dhf_ref, q_ref, k_ref, v_ref, wq_ref, wk_ref, wv_ref, dbias_ref, *rest):
    kv_out, q_out, (kv_sum, q_sum) = rest[:SIDE], rest[SIDE : SIDE + COLS], rest[SIDE + COLS :]
    pair = pl.program_id(0)
    rows, span = expo_ref.shape[1:]
    lane = lane_of((rows, 2 * SLOT))
    keys, values = k_ref[...], v_ref[...]
    d_q, d_k, d_v = [], 0.0, 0.0
    for i in range(2):
        mine = lane // SLOT == i
        d_head = jnp.where(mine, dhf_ref[...], 0)
        query = jnp.where(mine & (lane % SLOT < HD), q_ref[...], 0)
        expo = expo_ref[i]
        d_score = (expo.astype(F32) * nt(d_head, values)).astype(BF16)
        dbias_ref[i] = d_score
        d_q.append(nn(d_score, keys))
        d_k += tn(d_score, query)
        d_v += tn(expo, d_head)
    d_q = (jnp.where(lane < SLOT, d_q[0], d_q[1]) * (1.0 / math.sqrt(HD))).astype(BF16)
    d_kv = jnp.concatenate([(d_k * LN2).astype(BF16), d_v.astype(BF16)], axis=1)
    w_kv = jnp.concatenate([wk_ref[...], wv_ref[...]], axis=1)
    to_kv, to_q = nt(d_kv, w_kv), nt(d_q, wq_ref[...])

    @pl.when(pair == 0)
    def _():
        kv_sum[...] = to_kv
        q_sum[...] = to_q

    @pl.when(pair > 0)
    def _():
        kv_sum[...] += to_kv
        q_sum[...] += to_q

    @pl.when(pair == PAIRS - 1)
    def _():
        for sums, at, outs in ((kv_sum, yat_ref, kv_out), (q_sum, cat_ref, q_out)):
            size = outs[0].shape[0]
            for n, out in enumerate(outs):
                out[...] = sums[pl.ds(pl.multiple_of(at[n], size), size), :].astype(BF16)


def backward(yat, cat, expo, dhf, q, k, v, wq, wk, wv):
    rows, span = expo.shape[1:]
    width = wq.shape[0]
    wide = lambda n: pl.BlockSpec((n, 2 * SLOT), lambda p: (0, p))
    still = lambda *s: pl.BlockSpec(s, lambda p: (0,) * len(s))
    tile = pl.BlockSpec((2, rows, span), lambda p: (p, 0, 0))
    return pl.pallas_call(
        backward_kernel,
        grid=(PAIRS,),
        out_shape=[jax.ShapeDtypeStruct(expo.shape, BF16)]
        + [jax.ShapeDtypeStruct((span // SIDE, width), BF16)] * SIDE
        + [jax.ShapeDtypeStruct((rows // COLS, width), BF16)] * COLS,
        in_specs=[SCALAR, SCALAR, tile, wide(rows), wide(rows), wide(span), wide(span), wide(width), wide(width), wide(width)],
        out_specs=[tile] + [still(span // SIDE, width)] * SIDE + [still(rows // COLS, width)] * COLS,
        scratch_shapes=[pltpu.VMEM((span, width), F32), pltpu.VMEM((rows, width), F32)],
        compiler_params=params(),
        cost_estimate=pl.CostEstimate(flops=8 * HEADS * rows * span * 256, bytes_accessed=4 * HEADS * rows * span, transcendentals=0),
    )(yat, cat, expo, dhf, q, k, v, wq, wk, wv)


def reduce_kernel(at_ref, *refs):
    terms, outs, total = refs[:SIDE], refs[SIDE:-1], refs[-1]
    total[...] = functools.reduce(jnp.add, [t[...].astype(F32) for t in terms])
    size = outs[0].shape[0]
    for n, out in enumerate(outs):
        out[...] = total[pl.ds(pl.multiple_of(at_ref[n], size), size), :].astype(BF16)


def reduce_split(at, terms):
    rows, width = terms[0].shape
    return pl.pallas_call(
        reduce_kernel,
        out_shape=[jax.ShapeDtypeStruct((rows // SIDE, width), BF16)] * SIDE,
        in_specs=[SCALAR] + whole(SIDE),
        out_specs=whole(SIDE),
        scratch_shapes=[pltpu.VMEM((rows, width), F32)],
        compiler_params=params(),
    )(at, *terms)


def finish_kernel(at_ref, *refs):
    pieces, (gate_ref, dh_ref, wo_ref, wg_ref, att_ref, dg_ref) = refs[:COLS], refs[COLS:]
    size = pieces[0].shape[0]
    rows = pl.ds(pl.multiple_of(at_ref[0], size), size)
    out = functools.reduce(jnp.add, [p[...].astype(F32) for p in pieces])
    gate = gate_ref[rows, :]
    att_ref[...] = nn((out * gate).astype(BF16), wo_ref[...]).astype(BF16)
    d_gate = (dh_ref[rows, :] * out * (1.0 - gate)).astype(BF16)
    dg_ref[...] = nt(d_gate, wg_ref[...])


def finish(at, pieces, gate, dh, wo, wg):
    size, width = pieces[0].shape[0], wo.shape[1]
    return pl.pallas_call(
        finish_kernel,
        out_shape=[jax.ShapeDtypeStruct((size, width), BF16), jax.ShapeDtypeStruct((size, width), F32)],
        in_specs=[SCALAR] + whole(COLS + 4),
        out_specs=whole(2),
        compiler_params=params(),
    )(at, *pieces, gate, dh, wo, wg)


def send(pieces, axis, way):
    return [pieces[0]] + [lax.ppermute(pieces[k], axis, way(k)) for k in range(1, len(pieces))]


def widen(weight):
    split = weight.reshape(weight.shape[0], HEADS, HD)
    return jnp.pad(split, ((0, 0), (0, 0), (0, SLOT - HD))).reshape(weight.shape[0], WIDE)


def shards(single, pair_bias, key_live, w_query, w_key, w_value, w_gate, w_out, cotangent):
    rows, width = single.shape
    span = pair_bias.shape[2]
    piece = rows // COLS
    row_index, col_index = lax.axis_index("row"), lax.axis_index("col")
    y, x = row_index // SIDE, row_index % SIDE
    steps4, steps8 = jnp.arange(SIDE), jnp.arange(COLS)
    x_from, x_to = (x - steps4) % SIDE * (span // ROWS), (x + steps4) % SIDE * (span // ROWS)
    y_from, y_to = (y - steps4) % SIDE * (span // SIDE), (y + steps4) % SIDE * (span // SIDE)
    c_from, c_to = (col_index - steps8) % COLS * piece, (col_index + steps8) % COLS * piece

    mine = lax.dynamic_slice_in_dim(single, col_index * piece, piece, 0)
    mine = lax.ppermute(mine, ("row", "col"), home_to_block())
    line = place(send([mine] * SIDE, "row", along_x), x_from)
    lines = send([line] * SIDE, "row", along_y)

    wq, wk, wv, wg = (widen(w) for w in (w_query, w_key, w_value, w_gate))
    wo = jnp.pad(w_out.reshape(HEADS, HD, width), ((0, 0), (0, SLOT - HD), (0, 0))).reshape(WIDE, width)
    spot = lane_of((1, WIDE)) % SLOT
    scale = LOG2E / math.sqrt(HD)
    q = jnp.where((spot >= HD) & (spot < HD + 3), 1.0, nn(single, wq) * scale).astype(BF16)
    gate = jax.nn.sigmoid(nn(single, wg))
    dh = jnp.where(spot >= HD, 1.0, nt(cotangent, wo) * gate)
    alive = key_live > 0
    row = jnp.broadcast_to(jnp.where(alive, LOG2E, 0.0).astype(F32)[None, :], (8, span))
    live = jnp.broadcast_to(alive[:, None], (span, 2 * SLOT)).astype(BF16)
    rest, fill = jnp.float32(-30000.0 * LOG2E), jnp.zeros((1, 2 * SLOT), F32)
    for n in range(3):
        part = rest.astype(BF16).astype(F32)
        rest = rest - part
        fill = jnp.where(spot[:, : 2 * SLOT] == HD + n, part, fill)
    dead = jnp.where(alive[:, None], 0.0, fill).astype(BF16)

    k, v = project(lines, y_from, wk, wv)
    expo, acc, stats = forward(pair_bias, q, k, v, live, dead, row, dh)
    all_stats = send([stats] * COLS, "col", along_col)
    dhf, *parts = combine(c_to, all_stats, acc, dh)
    parts = send(parts, "col", along_col)
    d_bias, *outs = backward(y_to, c_to, expo, dhf, q, k, v, wq, wk, wv)
    attended, from_gate = finish(c_to, parts, gate, dh, wo, wg)
    attended = place(send([attended] * COLS, "col", along_col), c_from)
    from_kv, from_q = outs[:SIDE], outs[SIDE:]
    from_kv = reduce_split(x_to, send(from_kv, "row", along_y))
    from_kv = send(from_kv, "row", along_x)
    from_kv = functools.reduce(jnp.add, [p.astype(F32) for p in from_kv]).astype(BF16)
    back = [(b, a) for a, b in home_to_block()]
    from_kv = lax.ppermute(from_kv, ("row", "col"), back)
    from_q = send(from_q, "col", along_col)
    d_single = functools.reduce(jnp.add, [p.astype(F32) for p in from_q])
    d_single = (d_single + from_kv.astype(F32) + from_gate).astype(BF16)
    d_single = place(send([d_single] * COLS, "col", along_col), c_from)
    return (attended, d_bias, d_single)


def solution(mesh):
    placed = (
        P("row", None),
        P(None, "row", "col"),
        P("col"),
        P(),
        P(),
        P(),
        P(),
        P(),
        P("row", None),
    )
    return jax.shard_map(
        shards,
        mesh=mesh,
        in_specs=placed,
        out_specs=(P("row", None), P(None, "row", "col"), P("row", None)),
        check_vma=False,
    )
```

```python
import functools
import math

import jax
import jax.numpy as jnp
from jax import lax
from jax.experimental import pallas as pl
from jax.experimental.pallas import tpu as pltpu
from jax.sharding import PartitionSpec as P

HEADS = 16
HD = 48
EXTRA = 16
SLOT = HD + EXTRA
LOG2E = math.log2(math.e)
LN2 = math.log(2.0)
ROWS, COLS, SIDE = 16, 8, 4
VMEM = 56 * 1024 * 1024
F32, BF16 = jnp.float32, jnp.bfloat16


def dot(left, right, dims):
    return lax.dot_general(left, right, (dims, ((), ())), preferred_element_type=F32)


def nn(left, right):
    return dot(left, right, ((1,), (0,)))


def nt(left, right):
    return dot(left, right, ((1,), (1,)))


def tn(left, right):
    return dot(left, right, ((0,), (0,)))


def along_z(k):
    return [(z * 2 + core, (z + k) % SIDE * 2 + core) for z in range(SIDE) for core in range(2)]


def other_core():
    return [(c, c ^ 1) for c in range(COLS)]


def home_to_block():
    half = ROWS // 2
    return [
        (row * COLS + col, ((row % 2) * half + col) * COLS + row // 2)
        for row in range(ROWS)
        for col in range(COLS)
    ]


def params(**more):
    return pltpu.CompilerParams(vmem_limit_bytes=VMEM, **more)


def whole(count):
    return [pl.BlockSpec(memory_space=pltpu.VMEM)] * count


SCALAR = pl.BlockSpec(memory_space=pltpu.SMEM)
HBM = pl.BlockSpec(memory_space=pl.ANY)


def array(shape, dtype):
    return jax.ShapeDtypeStruct(shape, dtype)


def rows_at(start, size):
    return pl.ds(pl.multiple_of(start, 16), size)


def place_kernel(first, at_ref, *refs):
    *pieces, out = refs
    for k, piece in enumerate(pieces):
        out[rows_at(at_ref[first + k], piece.shape[0]), :] = piece[...]


def place(at, first, pieces):
    rows = sum(p.shape[0] for p in pieces)
    return pl.pallas_call(
        functools.partial(place_kernel, first),
        out_shape=array((rows, pieces[0].shape[1]), pieces[0].dtype),
        in_specs=[SCALAR] + whole(len(pieces)),
        out_specs=whole(1)[0],
        compiler_params=params(),
    )(at, *pieces)


def copier(sems):
    count = iter(range(sems.shape[0]))

    def start(source, target):
        copy = pltpu.make_async_copy(source, target, sems.at[next(count)])
        copy.start()
        return copy

    return start


GROUP = 4


def forward_kernel(*refs):
    tokens_hbm, bias_hbm, q_hbm, w_hbm, mask_hbm, row_hbm, dh_hbm, expo_hbm, kv_hbm, num_hbm, stats_ref = refs[:11]
    tokens, w_ref, q_ref, mask_ref, row_ref, dh_ref, bias_ref, kv_ref, expo_ref, num_ref, tops, sems = refs[11:]
    start = copier(sems)
    rows, width = q_ref.shape[1], w_ref.shape[1]
    early = [start(tokens_hbm, tokens), start(w_hbm, w_ref)]
    late = [start(a, b) for a, b in ((q_hbm, q_ref), (mask_hbm, mask_ref), (row_hbm, row_ref), (dh_hbm, dh_ref))]
    bias_in = [start(bias_hbm.at[h], bias_ref.at[h]) for h in range(HEADS)]
    for copy in early:
        copy.wait()
    out = []
    for part in range(4):
        span = slice(part * width // 2, (part + 1) * width // 2)
        kv_ref[span, :] = nt(w_ref[span, :], tokens[...]).astype(BF16)
        out.append(start(kv_ref.at[span], kv_hbm.at[span]))
    tops[...] = jnp.zeros_like(tops)
    for copy in late:
        copy.wait()
    ones_k = jnp.ones((EXTRA, tokens.shape[0]), BF16)
    ones_q = jnp.ones((EXTRA, rows), BF16)
    live, dead = mask_ref[:HD, :], mask_ref[HD:, :]

    def head(h):
        mine = slice(h * HD, (h + 1) * HD)
        keys = jnp.concatenate([kv_ref[mine, :] * live, dead], axis=0)
        query = jnp.concatenate([q_ref[mine, :], ones_q], axis=0)
        scores = tn(query, keys) + bias_ref[h].astype(F32) * row_ref[0:1, :]
        top = jnp.max(scores, axis=-1, keepdims=True)
        expo = jnp.exp2(scores - top).astype(BF16)
        expo_ref[h] = expo
        values = jnp.concatenate([kv_ref[width + h * HD : width + (h + 1) * HD, :], ones_k], axis=0)
        out = nt(values, expo)
        num = out[:HD]
        num_ref[mine, :] = num
        stats_ref[h : h + 1, :] = out[HD : HD + 1]
        stats_ref[2 * HEADS + h : 2 * HEADS + h + 1, :] = jnp.sum(num * dh_ref[mine, :].astype(F32), axis=0, keepdims=True)
        lane = lax.broadcasted_iota(jnp.int32, tops.shape, 1)
        tops[...] = jnp.where(lane == h, top, tops[...])

    for g in range(0, HEADS, GROUP):
        for h in range(g, g + GROUP):
            bias_in[h].wait()
        for h in range(g, g + GROUP):
            head(h)
        out.append(start(expo_ref.at[pl.ds(g, GROUP)], expo_hbm.at[pl.ds(g, GROUP)]))
        span = pl.ds(g * HD, GROUP * HD)
        out.append(start(num_ref.at[span], num_hbm.at[span]))

    stats_ref[HEADS : 2 * HEADS, :] = tops[...].T[:HEADS, :]
    for copy in out:
        copy.wait()


def forward(tokens, bias, q, w, mask, row, dh):
    rows, span = bias.shape[1:]
    width = w.shape[1]
    return pl.pallas_call(
        forward_kernel,
        out_shape=(
            array(bias.shape, BF16),
            array((2 * width, span), BF16),
            array((width, rows), F32),
            array((3 * HEADS, rows), F32),
        ),
        in_specs=[HBM] * 7,
        out_specs=(HBM, HBM, HBM, *whole(1)),
        scratch_shapes=[
            pltpu.VMEM((span, width), BF16),
            pltpu.VMEM(w.shape, BF16),
            pltpu.VMEM(q.shape, BF16),
            pltpu.VMEM(mask.shape, BF16),
            pltpu.VMEM(row.shape, F32),
            pltpu.VMEM(dh.shape, BF16),
            pltpu.VMEM(bias.shape, BF16),
            pltpu.VMEM((2 * width, span), BF16),
            pltpu.VMEM(bias.shape, BF16),
            pltpu.VMEM((width, rows), F32),
            pltpu.VMEM((rows, 128), F32),
            pltpu.SemaphoreType.DMA((64,)),
        ],
        compiler_params=params(),
        cost_estimate=pl.CostEstimate(flops=4 * HEADS * rows * span * 256, bytes_accessed=4 * HEADS * rows * span, transcendentals=HEADS * rows * span),
    )(tokens, bias, q, w, mask, row, dh)


def merge(stats):
    top = functools.reduce(jnp.maximum, [s[HEADS : 2 * HEADS, :] for s in stats])
    total, inner = jnp.zeros_like(top), jnp.zeros_like(top)
    for s in stats:
        weight = jnp.exp2(s[HEADS : 2 * HEADS, :] - top)
        total += weight * s[:HEADS, :]
        inner += weight * s[2 * HEADS :, :]
    return total, top, inner


def merge_kernel(left_ref, right_ref, out_ref):
    for n, part in enumerate(merge([left_ref[...], right_ref[...]])):
        out_ref[n * HEADS : (n + 1) * HEADS, :] = part


def merge_pair(left, right):
    return pl.pallas_call(
        merge_kernel,
        out_shape=array(left.shape, F32),
        in_specs=whole(2),
        out_specs=whole(1)[0],
        compiler_params=params(),
    )(left, right)


def combine_kernel(*refs):
    stats, (own_ref, num_ref, dh_ref, dhf_ref, out_ref) = refs[:SIDE], refs[SIDE:]
    total, top, inner = merge([s[...] for s in stats])
    factor = jnp.exp2(own_ref[HEADS : 2 * HEADS, :] - top) / total
    shift = -factor * (inner / total)
    row = lax.broadcasted_iota(jnp.int32, (EXTRA, shift.shape[1]), 0)
    for h in range(HEADS):
        span = slice(h * HD, (h + 1) * HD)
        scale = factor[h : h + 1, :]
        dhf_ref[h * SLOT : h * SLOT + HD, :] = (dh_ref[span, :].astype(F32) * scale).astype(BF16)
        out_ref[span, :] = num_ref[span, :] * scale
        rest, rows = shift[h : h + 1, :], 0.0
        for n in range(3):
            part = rest.astype(BF16).astype(F32)
            rest = rest - part
            rows = jnp.where(row == n, part, rows)
        dhf_ref[h * SLOT + HD : (h + 1) * SLOT, :] = rows.astype(BF16)


def combine(stats, own, num, dh):
    width, rows = num.shape
    return pl.pallas_call(
        combine_kernel,
        out_shape=(array((HEADS * SLOT, rows), BF16), array((width, rows), F32)),
        in_specs=whole(SIDE + 3),
        out_specs=tuple(whole(2)),
        compiler_params=params(),
    )(*stats, own, num, dh)


def backward_kernel(expo_hbm, dhf_hbm, q_hbm, kv_hbm, w_hbm, dbias_hbm, dq_hbm, sent_ref, *refs):
    expo_ref, dhf_ref, q_ref, kv_ref, w_ref, dbias_ref, dq_ref, dkv, sems = refs
    start = copier(sems)
    width = q_ref.shape[0]
    early = [start(a, b) for a, b in ((dhf_hbm, dhf_ref), (kv_hbm, kv_ref), (q_hbm, q_ref))]
    expo_in = [start(expo_hbm.at[h], expo_ref.at[h]) for h in range(HEADS)]
    late = start(w_hbm, w_ref)
    for copy in early:
        copy.wait()
    ones_k = jnp.ones((EXTRA, kv_ref.shape[1]), BF16)

    def head(h):
        mine, other = slice(h * HD, (h + 1) * HD), slice(width + h * HD, width + (h + 1) * HD)
        values = jnp.concatenate([kv_ref[other, :], ones_k], axis=0)
        expo = expo_ref[h]
        d_score = (expo.astype(F32) * tn(dhf_ref[h * SLOT : (h + 1) * SLOT, :], values)).astype(BF16)
        dbias_ref[h] = d_score
        dq_ref[mine, :] = (nt(kv_ref[mine, :], d_score) * (1.0 / math.sqrt(HD))).astype(BF16)
        dkv[mine, :] = (nn(q_ref[mine, :], d_score) * LN2).astype(BF16)
        dkv[other, :] = nn(dhf_ref[h * SLOT : h * SLOT + HD, :], expo).astype(BF16)

    out = []
    for g in range(0, HEADS, GROUP):
        for h in range(g, g + GROUP):
            expo_in[h].wait()
        for h in range(g, g + GROUP):
            head(h)
        out.append(start(dbias_ref.at[pl.ds(g, GROUP)], dbias_hbm.at[pl.ds(g, GROUP)]))
    out.append(start(dq_ref, dq_hbm))
    late.wait()
    sent_ref[...] = tn(dkv[...], w_ref[...]).astype(BF16)
    for copy in out:
        copy.wait()


def backward(expo, dhf, q, kv, w):
    rows, span = expo.shape[1:]
    width = q.shape[0]
    return pl.pallas_call(
        backward_kernel,
        out_shape=[array(expo.shape, BF16), array(q.shape, BF16), array((span, width), BF16)],
        in_specs=[HBM] * 5,
        out_specs=[HBM, HBM, *whole(1)],
        scratch_shapes=[
            pltpu.VMEM(expo.shape, BF16),
            pltpu.VMEM(dhf.shape, BF16),
            pltpu.VMEM(q.shape, BF16),
            pltpu.VMEM(kv.shape, BF16),
            pltpu.VMEM(w.shape, BF16),
            pltpu.VMEM(expo.shape, BF16),
            pltpu.VMEM(q.shape, BF16),
            pltpu.VMEM((2 * width, span), BF16),
            pltpu.SemaphoreType.DMA((64,)),
        ],
        compiler_params=params(),
        cost_estimate=pl.CostEstimate(flops=8 * HEADS * rows * span * 256, bytes_accessed=4 * HEADS * rows * span, transcendentals=0),
    )(expo, dhf, q, kv, w)


def prepare_kernel(single_ref, cot_ref, wq_ref, wg_ref, wo_ref, q_ref, dh_ref):
    single = single_ref[...]
    q_ref[...] = (dot(wq_ref[...], single, ((0,), (1,))) * (LOG2E / math.sqrt(HD))).astype(BF16)
    gate = jax.nn.sigmoid(dot(wg_ref[...], single, ((0,), (1,))))
    dh_ref[...] = (nt(wo_ref[...], cot_ref[...]) * gate).astype(BF16)


def prepare(single, cotangent, wq, wg, wo):
    rows, width = single.shape
    return pl.pallas_call(
        prepare_kernel,
        out_shape=(array((width, rows), BF16), array((width, rows), BF16)),
        in_specs=whole(5),
        out_specs=tuple(whole(2)),
        compiler_params=params(),
    )(single, cotangent, wq, wg, wo)


def finish_kernel(*refs):
    parts, (single_ref, cot_ref, wo_ref, wg_ref, att_ref, rest_ref) = refs[:SIDE], refs[SIDE:]
    size = single_ref.shape[0]
    both = functools.reduce(jnp.add, [p[...].astype(F32) for p in parts])
    d_query, out = both[:size], both[size:]
    gate = jax.nn.sigmoid(nn(single_ref[...], wg_ref[...]))
    att_ref[...] = nn((out * gate).astype(BF16), wo_ref[...]).astype(BF16)
    d_gate = (nt(cot_ref[...], wo_ref[...]) * out * gate * (1.0 - gate)).astype(BF16)
    rest_ref[...] = d_query + nt(d_gate, wg_ref[...])


def finish(parts, single, cotangent, wo, wg):
    return pl.pallas_call(
        finish_kernel,
        out_shape=(array(single.shape, BF16), array(single.shape, F32)),
        in_specs=whole(SIDE + 4),
        out_specs=tuple(whole(2)),
        compiler_params=params(),
    )(*parts, single, cotangent, wo, wg)


def query_kernel(first, at_ref, dq_ref, out_ref, w_ref, mine_ref, other_ref, total, turned):
    total[...] = dot(dq_ref[...], w_ref[...], ((0,), (1,)))
    turned[...] = out_ref[...].T
    size = total.shape[0] // COLS
    for n, out in enumerate((mine_ref, other_ref)):
        for k in range(SIDE):
            rows = rows_at(at_ref[first + n * SIDE + k], size)
            out[2 * k * size : (2 * k + 1) * size, :] = total[rows, :].astype(BF16)
            out[(2 * k + 1) * size : (2 * k + 2) * size, :] = turned[rows, :].astype(BF16)


def query(at, first, dq, out, w):
    width, rows = dq.shape
    return pl.pallas_call(
        functools.partial(query_kernel, first),
        out_shape=[array((rows, width), BF16)] * 2,
        in_specs=[SCALAR] + whole(3),
        out_specs=whole(2),
        scratch_shapes=[pltpu.VMEM((rows, width), F32)] * 2,
        compiler_params=params(),
    )(at, dq, out, w)


def split_kernel(left_ref, right_ref, *outs):
    size = outs[0].shape[0]
    for n, out in enumerate(outs):
        rows = slice(n * size, (n + 1) * size)
        out[...] = (left_ref[rows, :].astype(F32) + right_ref[rows, :].astype(F32)).astype(BF16)


def add_split(terms):
    rows, width = terms[0].shape
    return pl.pallas_call(
        split_kernel,
        out_shape=[array((rows // SIDE, width), BF16)] * SIDE,
        in_specs=whole(2),
        out_specs=whole(SIDE),
        compiler_params=params(),
    )(*terms)


def total_kernel(attended_ref, kv_ref, rest_ref, out_ref):
    size = kv_ref.shape[0]
    out_ref[:size, :] = attended_ref[...]
    out_ref[size:, :] = (kv_ref[...].astype(F32) + rest_ref[...]).astype(BF16)


def total(attended, from_kv, rest):
    size, width = attended.shape
    return pl.pallas_call(
        total_kernel,
        out_shape=array((2 * size, width), BF16),
        in_specs=whole(3),
        out_specs=whole(1)[0],
        compiler_params=params(),
    )(attended, from_kv, rest)


def join_kernel(first, at_ref, own_ref, other_ref, *outs):
    size = own_ref.shape[0] // COLS
    mine = at_ref[first]
    for ref, shift in ((own_ref, mine), (other_ref, size - mine)):
        for n, out in enumerate(outs):
            for z in range(SIDE):
                source = slice((2 * z + n) * size, (2 * z + n + 1) * size)
                out[rows_at(2 * z * size + shift, size), :] = ref[source, :]


def join(at, first, own, other):
    rows, width = own.shape
    return pl.pallas_call(
        functools.partial(join_kernel, first),
        out_shape=[array((rows, width), BF16)] * 2,
        in_specs=[SCALAR] + whole(2),
        out_specs=whole(2),
        compiler_params=params(),
    )(at, own, other)


def shards(single, pair_bias, key_live, w_query, w_key, w_value, w_gate, w_out, cotangent):
    rows, width = single.shape
    span = pair_bias.shape[2]
    piece = rows // COLS
    col_index = lax.axis_index("col")
    z, core = col_index // 2, col_index % 2
    steps = jnp.arange(SIDE, dtype=jnp.int32)
    at = jnp.concatenate([
        ((z + steps) % SIDE * 2 + core) * piece,
        ((z + steps) % SIDE * 2 + 1 - core) * piece,
        (z - steps) % SIDE * 2 * piece,
        core[None] * piece,
    ]).astype(jnp.int32)
    both = ("row", "col")

    own = [lax.dynamic_slice_in_dim(a, col_index * piece, piece, 0) for a in (single, cotangent)]
    tokens = lax.ppermute(own[0], both, home_to_block())
    tokens = jnp.broadcast_to(tokens[None], (ROWS, piece, width))
    tokens = lax.all_to_all(tokens, "row", 0, 0).reshape(span, width)

    wkv = jnp.concatenate([w_key, w_value], axis=1).T
    q, dh = prepare(single, cotangent, w_query, w_gate, w_out)
    alive = key_live[None, :] > 0
    row = jnp.broadcast_to(jnp.where(alive, LOG2E, 0.0).astype(F32), (8, span))
    live = jnp.broadcast_to(alive, (HD, span)).astype(BF16)
    rest, spot = jnp.float32(-30000.0 * LOG2E), lax.broadcasted_iota(jnp.int32, (EXTRA, 1), 0)
    fill = jnp.zeros((EXTRA, 1), F32)
    for n in range(3):
        part = rest.astype(BF16).astype(F32)
        rest = rest - part
        fill = jnp.where(spot == n, part, fill)
    dead = jnp.where(alive, 0.0, fill).astype(BF16)

    mask = jnp.concatenate([live, dead], axis=0)
    expo, kv, num, stats = forward(tokens, pair_bias, q, wkv, mask, row, dh)
    chip = merge_pair(stats, lax.ppermute(stats, "col", other_core()))
    every = [chip] + [lax.ppermute(chip, "col", along_z(k)) for k in (1, 3, 2)]
    dhf, out = combine(every, stats, num, dh)
    d_bias, dq, from_kv = backward(expo, dhf, q, kv, wkv)

    from_kv = lax.all_to_all(from_kv.reshape(ROWS, piece, width), "row", 0, 0)
    from_kv = jnp.sum(from_kv.astype(F32), axis=0).astype(BF16)
    from_kv = lax.ppermute(from_kv, both, [(b, a) for a, b in home_to_block()])

    mine, other = query(at, 0, dq, out, w_query)
    other = lax.ppermute(other, "col", other_core())
    parts = add_split([mine, other])
    parts = [parts[0]] + [lax.ppermute(parts[k], "col", along_z(k)) for k in (1, 3, 2)]
    attended, rest = finish(parts, *own, w_out, w_gate)
    ends = total(attended, from_kv, rest)
    ends = place(at, 8, [ends] + [lax.ppermute(ends, "col", along_z(k)) for k in (1, 2, 3)])
    attended, d_single = join(at, 12, ends, lax.ppermute(ends, "col", other_core()))
    return (attended, d_bias, d_single)


def solution(mesh):
    placed = (
        P("row", None),
        P(None, "row", "col"),
        P("col"),
        P(),
        P(),
        P(),
        P(),
        P(),
        P("row", None),
    )
    return jax.shard_map(
        shards,
        mesh=mesh,
        in_specs=placed,
        out_specs=(P("row", None), P(None, "row", "col"), P("row", None)),
        check_vma=False,
    )
```

```python
import functools
import math

import jax
import jax.numpy as jnp
from jax import lax
from jax.experimental import pallas as pl
from jax.experimental.pallas import tpu as pltpu
from jax.sharding import PartitionSpec as P

HEADS = 16
HD = 48
EXTRA = 16
SLOT = HD + EXTRA
LOG2E = math.log2(math.e)
LN2 = math.log(2.0)
ROWS, COLS, SIDE = 16, 8, 4
VMEM = 56 * 1024 * 1024
F32, BF16 = jnp.float32, jnp.bfloat16


def dot(left, right, dims):
    return lax.dot_general(left, right, (dims, ((), ())), preferred_element_type=F32)


def nn(left, right):
    return dot(left, right, ((1,), (0,)))


def nt(left, right):
    return dot(left, right, ((1,), (1,)))


def tn(left, right):
    return dot(left, right, ((0,), (0,)))


def along_z(k):
    return [(z * 2 + core, (z + k) % SIDE * 2 + core) for z in range(SIDE) for core in range(2)]


def other_core():
    return [(c, c ^ 1) for c in range(COLS)]


def home_of(y, x, z, core):
    turn = (x - 2 * core) % SIDE
    return (turn + 1) % SIDE // 2, (z + 2 - (y - z)) % SIDE * 2 + turn // 2


def home_to_block():
    pairs = []
    for y in range(SIDE):
        for x in range(SIDE):
            for col in range(COLS):
                half, home = home_of(y, x, col // 2, col % 2)
                pairs.append(((2 * col + half) * COLS + home, (y * SIDE + x) * COLS + col))
    return pairs


def params(**more):
    return pltpu.CompilerParams(vmem_limit_bytes=VMEM, **more)


def whole(count):
    return [pl.BlockSpec(memory_space=pltpu.VMEM)] * count


SCALAR = pl.BlockSpec(memory_space=pltpu.SMEM)
HBM = pl.BlockSpec(memory_space=pl.ANY)


def array(shape, dtype):
    return jax.ShapeDtypeStruct(shape, dtype)


def rows_at(start, size):
    return pl.ds(pl.multiple_of(start, 16), size)


def copier(sems):
    count = iter(range(sems.shape[0]))

    def start(source, target):
        copy = pltpu.make_async_copy(source, target, sems.at[next(count)])
        copy.start()
        return copy

    return start


GROUP = 4
CHUNK = 32


def forward_kernel(first, at_ref, *refs):
    tokens_hbm, bias_hbm, q_hbm, w_hbm, mask_hbm, row_hbm, dh_hbm, expo_hbm, kv_hbm, num_hbm, stats_ref = refs[:11]
    tokens, w_ref, q_ref, mask_ref, row_ref, dh_ref, bias_ref, kv_ref, expo_ref, num_ref, tops, score_ref, sems = refs[-13:]
    start = copier(sems)
    rows, width = q_ref.shape[1], w_ref.shape[1]
    early = [start(w_hbm, w_ref)]
    for n in range(ROWS):
        early.append(start(tokens_hbm.at[n], tokens.at[rows_at(at_ref[first + n], tokens_hbm.shape[1])]))
    late = [start(a, b) for a, b in ((q_hbm, q_ref), (mask_hbm, mask_ref), (row_hbm, row_ref), (dh_hbm, dh_ref))]
    bias_in = [start(bias_hbm.at[h], bias_ref.at[h]) for h in range(HEADS)]
    for copy in early:
        copy.wait()
    out = []
    for part in range(4):
        span = slice(part * width // 2, (part + 1) * width // 2)
        kv_ref[span, :] = nt(w_ref[span, :], tokens[...]).astype(BF16)
        out.append(start(kv_ref.at[span], kv_hbm.at[span]))
    tops[...] = jnp.zeros_like(tops)
    for copy in late:
        copy.wait()
    ones_k = jnp.ones((EXTRA, tokens.shape[0]), BF16)
    ones_q = jnp.ones((EXTRA, rows), BF16)
    live, dead = mask_ref[:HD, :], mask_ref[HD:, :]

    def scores_of(h):
        mine = slice(h * HD, (h + 1) * HD)
        keys = jnp.concatenate([kv_ref[mine, :] * live, dead], axis=0)
        query = jnp.concatenate([q_ref[mine, :], ones_q], axis=0)
        score_ref[h % 2] = tn(query, keys)

    def soften(h):
        lane = lax.broadcasted_iota(jnp.int32, (CHUNK, 128), 1)
        for c in range(0, rows, CHUNK):
            part = slice(c, c + CHUNK)
            scores = score_ref[h % 2, part, :] + bias_ref[h, part, :].astype(F32) * row_ref[0:1, :]
            top = jnp.max(scores, axis=-1, keepdims=True)
            expo_ref[h, part, :] = jnp.exp2(scores - top).astype(BF16)
            tops[part, :] = jnp.where(lane == h, top, tops[part, :])

    def weigh(h):
        mine = slice(h * HD, (h + 1) * HD)
        values = jnp.concatenate([kv_ref[width + h * HD : width + (h + 1) * HD, :], ones_k], axis=0)
        sums = nt(values, expo_ref[h])
        num = sums[:HD]
        num_ref[mine, :] = num
        stats_ref[h : h + 1, :] = sums[HD : HD + 1]
        stats_ref[2 * HEADS + h : 2 * HEADS + h + 1, :] = jnp.sum(num * dh_ref[mine, :].astype(F32), axis=0, keepdims=True)

    scores_of(0)
    for h in range(HEADS):
        if h % GROUP == 0:
            for n in range(h, h + GROUP):
                bias_in[n].wait()
        if h + 1 < HEADS:
            scores_of(h + 1)
        if h:
            weigh(h - 1)
        soften(h)
        if h % GROUP == GROUP - 1:
            group = pl.ds(h + 1 - GROUP, GROUP)
            out.append(start(expo_ref.at[group], expo_hbm.at[group]))
    weigh(HEADS - 1)
    out.append(start(num_ref, num_hbm))

    stats_ref[HEADS : 2 * HEADS, :] = tops[...].T[:HEADS, :]
    for copy in out:
        copy.wait()


def forward(at, first, tokens, bias, q, w, mask, row, dh):
    rows, span = bias.shape[1:]
    width = w.shape[1]
    return pl.pallas_call(
        functools.partial(forward_kernel, first),
        out_shape=(
            array(bias.shape, BF16),
            array((2 * width, span), BF16),
            array((width, rows), F32),
            array((3 * HEADS, rows), F32),
        ),
        in_specs=[SCALAR] + [HBM] * 7,
        out_specs=(HBM, HBM, HBM, *whole(1)),
        scratch_shapes=[
            pltpu.VMEM((span, width), BF16),
            pltpu.VMEM(w.shape, BF16),
            pltpu.VMEM(q.shape, BF16),
            pltpu.VMEM(mask.shape, BF16),
            pltpu.VMEM(row.shape, F32),
            pltpu.VMEM(dh.shape, BF16),
            pltpu.VMEM(bias.shape, BF16),
            pltpu.VMEM((2 * width, span), BF16),
            pltpu.VMEM(bias.shape, BF16),
            pltpu.VMEM((width, rows), F32),
            pltpu.VMEM((rows, 128), F32),
            pltpu.VMEM((2, rows, span), F32),
            pltpu.SemaphoreType.DMA((64,)),
        ],
        compiler_params=params(),
        cost_estimate=pl.CostEstimate(flops=4 * HEADS * rows * span * 256, bytes_accessed=4 * HEADS * rows * span, transcendentals=HEADS * rows * span),
    )(at, tokens, bias, q, w, mask, row, dh)


def merge(stats):
    top = functools.reduce(jnp.maximum, [s[HEADS : 2 * HEADS, :] for s in stats])
    total, inner = jnp.zeros_like(top), jnp.zeros_like(top)
    for s in stats:
        weight = jnp.exp2(s[HEADS : 2 * HEADS, :] - top)
        total += weight * s[:HEADS, :]
        inner += weight * s[2 * HEADS :, :]
    return total, top, inner


def merge_kernel(left_ref, right_ref, out_ref):
    for n, part in enumerate(merge([left_ref[...], right_ref[...]])):
        out_ref[n * HEADS : (n + 1) * HEADS, :] = part


def merge_pair(left, right):
    return pl.pallas_call(
        merge_kernel,
        out_shape=array(left.shape, F32),
        in_specs=whole(2),
        out_specs=whole(1)[0],
        compiler_params=params(),
    )(left, right)


def backward_kernel(first, at_ref, *refs):
    stats, refs = refs[: SIDE + 1], refs[SIDE + 1 :]
    num_hbm, dh_hbm, expo_hbm, q_hbm, kv_hbm, w_hbm, dbias_hbm, dq_hbm, sent_hbm, out_hbm = refs[:10]
    num_ref, dh_ref, out_ref, expo_ref, dhf_ref, q_ref, kv_ref, w_ref, dbias_ref, dq_ref, dkv, prod_ref, sums, sems = refs[10:]
    start = copier(sems)
    width = q_ref.shape[0]
    early = [start(a, b) for a, b in ((dh_hbm, dh_ref), (num_hbm, num_ref), (kv_hbm, kv_ref), (q_hbm, q_ref))]
    expo_in = [start(expo_hbm.at[h], expo_ref.at[h]) for h in range(HEADS)]
    late = start(w_hbm, w_ref)
    total, top, inner = merge([s[...] for s in stats[1:]])
    factor = jnp.exp2(stats[0][HEADS : 2 * HEADS, :] - top) / total
    shift = -factor * (inner / total)
    row = lax.broadcasted_iota(jnp.int32, (EXTRA, shift.shape[1]), 0)
    for copy in early:
        copy.wait()
    ones_k = jnp.ones((EXTRA, kv_ref.shape[1]), BF16)

    def combine(h):
        mine, scale = slice(h * HD, (h + 1) * HD), factor[h : h + 1, :]
        dhf_ref[h * SLOT : h * SLOT + HD, :] = (dh_ref[mine, :].astype(F32) * scale).astype(BF16)
        out_ref[mine, :] = num_ref[mine, :] * scale
        rest, rows = shift[h : h + 1, :], 0.0
        for n in range(3):
            part = rest.astype(BF16).astype(F32)
            rest = rest - part
            rows = jnp.where(row == n, part, rows)
        dhf_ref[h * SLOT + HD : (h + 1) * SLOT, :] = rows.astype(BF16)

    def products(h):
        values = jnp.concatenate([kv_ref[width + h * HD : width + (h + 1) * HD, :], ones_k], axis=0)
        prod_ref[h % 2] = tn(dhf_ref[h * SLOT : (h + 1) * SLOT, :], values)

    def scores(h):
        for c in range(0, prod_ref.shape[1], CHUNK):
            part = slice(c, c + CHUNK)
            dbias_ref[h, part, :] = (expo_ref[h, part, :].astype(F32) * prod_ref[h % 2, part, :]).astype(BF16)

    def to_values(h):
        other = slice(width + h * HD, width + (h + 1) * HD)
        dkv[other, :] = nn(dhf_ref[h * SLOT : h * SLOT + HD, :], expo_ref[h]).astype(BF16)

    def to_queries_and_keys(h):
        mine, d_score = slice(h * HD, (h + 1) * HD), dbias_ref[h]
        dq_ref[mine, :] = (nt(kv_ref[mine, :], d_score) * (1.0 / math.sqrt(HD))).astype(BF16)
        dkv[mine, :] = (nn(q_ref[mine, :], d_score) * LN2).astype(BF16)

    out = []
    combine(0)
    products(0)
    for h in range(HEADS):
        if h % GROUP == 0:
            for n in range(h, h + GROUP):
                expo_in[n].wait()
        if h + 1 < HEADS:
            combine(h + 1)
            products(h + 1)
        to_values(h)
        if h:
            to_queries_and_keys(h - 1)
        scores(h)
        if h % GROUP == GROUP - 1:
            group = pl.ds(h + 1 - GROUP, GROUP)
            out.append(start(dbias_ref.at[group], dbias_hbm.at[group]))
    to_queries_and_keys(HEADS - 1)
    out.append(start(dq_ref, dq_hbm))
    out.append(start(out_ref, out_hbm))
    late.wait()
    sums[...] = tn(dkv[...], w_ref[...]).astype(BF16)
    size = sums.shape[0] // ROWS
    for n in range(ROWS):
        out.append(start(sums.at[rows_at(at_ref[first + n], size)], sent_hbm.at[n]))
    for copy in out:
        copy.wait()


def backward(at, first, own, every, num, dh, expo, q, kv, w):
    rows, span = expo.shape[1:]
    width = q.shape[0]
    return pl.pallas_call(
        functools.partial(backward_kernel, first),
        out_shape=[array(expo.shape, BF16), array(q.shape, BF16), array((ROWS, span // ROWS, width), BF16), array(num.shape, F32)],
        in_specs=[SCALAR] + whole(SIDE + 1) + [HBM] * 6,
        out_specs=[HBM] * 4,
        scratch_shapes=[
            pltpu.VMEM(num.shape, F32),
            pltpu.VMEM(dh.shape, BF16),
            pltpu.VMEM(num.shape, F32),
            pltpu.VMEM(expo.shape, BF16),
            pltpu.VMEM((HEADS * SLOT, rows), BF16),
            pltpu.VMEM(q.shape, BF16),
            pltpu.VMEM(kv.shape, BF16),
            pltpu.VMEM(w.shape, BF16),
            pltpu.VMEM(expo.shape, BF16),
            pltpu.VMEM(q.shape, BF16),
            pltpu.VMEM((2 * width, span), BF16),
            pltpu.VMEM((2, rows, span), F32),
            pltpu.VMEM((span, width), BF16),
            pltpu.SemaphoreType.DMA((64,)),
        ],
        compiler_params=params(),
        cost_estimate=pl.CostEstimate(flops=8 * HEADS * rows * span * 256, bytes_accessed=4 * HEADS * rows * span, transcendentals=0),
    )(at, own, *every, num, dh, expo, q, kv, w)


def prepare_kernel(single_ref, cot_ref, own_ref, own_cot_ref, wq_ref, wg_ref, wo_ref, q_ref, dh_ref, gate_ref, dhid_ref):
    single = single_ref[...]
    q_ref[...] = (dot(wq_ref[...], single, ((0,), (1,))) * (LOG2E / math.sqrt(HD))).astype(BF16)
    gate = jax.nn.sigmoid(dot(wg_ref[...], single, ((0,), (1,))))
    dh_ref[...] = (nt(wo_ref[...], cot_ref[...]) * gate).astype(BF16)
    gate_ref[...] = jax.nn.sigmoid(nn(own_ref[...], wg_ref[...]))
    dhid_ref[...] = nt(own_cot_ref[...], wo_ref[...])


def prepare(single, cotangent, own, wq, wg, wo):
    rows, width = single.shape
    return pl.pallas_call(
        prepare_kernel,
        out_shape=[array((width, rows), BF16)] * 2 + [array(own[0].shape, F32)] * 2,
        in_specs=whole(7),
        out_specs=whole(4),
        compiler_params=params(),
    )(single, cotangent, *own, wq, wg, wo)


def finish_kernel(*refs):
    parts, (gate_ref, dhid_ref, wo_ref, wg_ref, out_ref) = refs[:SIDE], refs[SIDE:]
    size = gate_ref.shape[0]
    both = functools.reduce(jnp.add, [p[...].astype(F32) for p in parts])
    d_query, out, gate = both[:size], both[size:], gate_ref[...]
    out_ref[:size, :] = nn((out * gate).astype(BF16), wo_ref[...]).astype(BF16)
    d_gate = (dhid_ref[...] * out * gate * (1.0 - gate)).astype(BF16)
    out_ref[size:, :] = (d_query + nt(d_gate, wg_ref[...])).astype(BF16)


def finish(parts, gate, d_hidden, wo, wg):
    return pl.pallas_call(
        finish_kernel,
        out_shape=array(parts[0].shape, BF16),
        in_specs=whole(SIDE + 4),
        out_specs=whole(1)[0],
        compiler_params=params(),
    )(*parts, gate, d_hidden, wo, wg)


def query_kernel(first, at_ref, dq_ref, out_ref, w_ref, mine_ref, other_ref, total, turned):
    total[...] = dot(dq_ref[...], w_ref[...], ((0,), (1,)))
    turned[...] = out_ref[...].T
    size = total.shape[0] // COLS
    for n, out in enumerate((mine_ref, other_ref)):
        for k in range(SIDE):
            rows = rows_at(at_ref[first + n * SIDE + k], size)
            out[2 * k * size : (2 * k + 1) * size, :] = total[rows, :].astype(BF16)
            out[(2 * k + 1) * size : (2 * k + 2) * size, :] = turned[rows, :].astype(BF16)


def query(at, first, dq, out, w):
    width, rows = dq.shape
    return pl.pallas_call(
        functools.partial(query_kernel, first),
        out_shape=[array((rows, width), BF16)] * 2,
        in_specs=[SCALAR] + whole(3),
        out_specs=whole(2),
        scratch_shapes=[pltpu.VMEM((rows, width), F32)] * 2,
        compiler_params=params(),
    )(at, dq, out, w)


def split_kernel(left_ref, right_ref, *outs):
    size = outs[0].shape[0]
    for n, out in enumerate(outs):
        rows = slice(n * size, (n + 1) * size)
        out[...] = (left_ref[rows, :].astype(F32) + right_ref[rows, :].astype(F32)).astype(BF16)


def add_split(terms):
    rows, width = terms[0].shape
    return pl.pallas_call(
        split_kernel,
        out_shape=[array((rows // SIDE, width), BF16)] * SIDE,
        in_specs=whole(2),
        out_specs=whole(SIDE),
        compiler_params=params(),
    )(*terms)


def total_kernel(kv_ref, ends_ref, out_ref):
    size = kv_ref.shape[0]
    out_ref[:size, :] = ends_ref[:size, :]
    out_ref[size:, :] = (ends_ref[size:, :].astype(F32) + kv_ref[...].astype(F32)).astype(BF16)


def total(from_kv, ends):
    return pl.pallas_call(
        total_kernel,
        out_shape=array(ends.shape, BF16),
        in_specs=whole(2),
        out_specs=whole(1)[0],
        compiler_params=params(),
    )(from_kv, ends)


def join_kernel(first, at_ref, *refs):
    ends, outs = refs[: 2 * SIDE], refs[2 * SIDE :]
    size = ends[0].shape[0] // 2
    core = at_ref[first + SIDE]
    for k, end in enumerate(ends):
        shift = core if k < SIDE else size - core
        for n, out in enumerate(outs):
            out[rows_at(at_ref[first + k % SIDE] + shift, size), :] = end[n * size : (n + 1) * size, :]


def join(at, first, near, far):
    size, width = near[0].shape
    return pl.pallas_call(
        functools.partial(join_kernel, first),
        out_shape=[array((size // 2 * COLS, width), BF16)] * 2,
        in_specs=[SCALAR] + whole(COLS),
        out_specs=whole(2),
        compiler_params=params(),
    )(at, *near, *far)


def shards(single, pair_bias, key_live, w_query, w_key, w_value, w_gate, w_out, cotangent):
    rows, width = single.shape
    span = pair_bias.shape[2]
    piece = rows // COLS
    col_index = lax.axis_index("col")
    z, core = col_index // 2, col_index % 2
    steps = jnp.arange(SIDE, dtype=jnp.int32)
    at = jnp.concatenate([
        ((z + steps) % SIDE * 2 + core) * piece,
        ((z + steps) % SIDE * 2 + 1 - core) * piece,
        (z - steps) % SIDE * 2 * piece,
        core[None] * piece,
        jnp.stack([half * rows + home * piece for y in range(SIDE) for x in range(SIDE) for half, home in [home_of(y, x, z, core)]]),
    ]).astype(jnp.int32)
    both = ("row", "col")

    own = [lax.dynamic_slice_in_dim(a, col_index * piece, piece, 0) for a in (single, cotangent)]
    tokens = lax.ppermute(own[0], both, home_to_block())
    tokens = lax.all_to_all(jnp.broadcast_to(tokens[None], (ROWS, *tokens.shape)), "row", 0, 0)
    wkv = jnp.concatenate([w_key, w_value], axis=1).T
    q, dh, gate, d_hidden = prepare(single, cotangent, own, w_query, w_gate, w_out)
    alive = key_live[None, :] > 0
    row = jnp.broadcast_to(jnp.where(alive, LOG2E, 0.0).astype(F32), (8, span))
    live = jnp.broadcast_to(alive, (HD, span)).astype(BF16)
    rest, spot = jnp.float32(-30000.0 * LOG2E), lax.broadcasted_iota(jnp.int32, (EXTRA, 1), 0)
    fill = jnp.zeros((EXTRA, 1), F32)
    for n in range(3):
        part = rest.astype(BF16).astype(F32)
        rest = rest - part
        fill = jnp.where(spot == n, part, fill)
    dead = jnp.where(alive, 0.0, fill).astype(BF16)

    mask = jnp.concatenate([live, dead], axis=0)
    expo, kv, num, stats = forward(at, 13, tokens, pair_bias, q, wkv, mask, row, dh)
    chip = merge_pair(stats, lax.ppermute(stats, "col", other_core()))
    every = [chip] + [lax.ppermute(chip, "col", along_z(k)) for k in (1, 3, 2)]
    d_bias, dq, from_kv, out = backward(at, 13, stats, every, num, dh, expo, q, kv, wkv)

    from_kv = lax.all_to_all(from_kv, "row", 0, 0)
    mine, other = query(at, 0, dq, out, w_query)
    other = lax.ppermute(other, "col", other_core())
    parts = add_split([mine, other])
    parts = [parts[0]] + [lax.ppermute(parts[k], "col", along_z(k)) for k in (1, 3, 2)]
    ends = finish(parts, gate, d_hidden, w_out, w_gate)
    from_kv = jnp.sum(from_kv.astype(F32), axis=0).astype(BF16)
    from_kv = lax.ppermute(from_kv, both, [(b, a) for a, b in home_to_block()])
    ends = total(from_kv, ends)
    near = [ends] + [lax.ppermute(ends, "col", along_z(k)) for k in (1, 2, 3)]
    far = [lax.ppermute(end, "col", other_core()) for end in near]
    attended, d_single = join(at, 8, near, far)
    return (attended, d_bias, d_single)


def solution(mesh):
    placed = (
        P("row", None),
        P(None, "row", "col"),
        P("col"),
        P(),
        P(),
        P(),
        P(),
        P(),
        P("row", None),
    )
    return jax.shard_map(
        shards,
        mesh=mesh,
        in_specs=placed,
        out_specs=(P("row", None), P(None, "row", "col"), P("row", None)),
        check_vma=False,
    )
```

```python
import functools
import math

import jax
import jax.numpy as jnp
from jax import lax
from jax.experimental import pallas as pl
from jax.experimental.pallas import tpu as pltpu
from jax.sharding import PartitionSpec as P

HEADS = 16
HD = 48
EXTRA = 16
SLOT = HD + EXTRA
LOG2E = math.log2(math.e)
LN2 = math.log(2.0)
ROWS, COLS, SIDE = 16, 8, 4
F32, BF16 = jnp.float32, jnp.bfloat16


def dot(left, right, dims):
    return lax.dot_general(left, right, (dims, ((), ())), preferred_element_type=F32)


def nn(left, right):
    return dot(left, right, ((1,), (0,)))


def nt(left, right):
    return dot(left, right, ((1,), (1,)))


def tn(left, right):
    return dot(left, right, ((0,), (0,)))


def along_z(k):
    return [(z * 2 + core, (z + k) % SIDE * 2 + core) for z in range(SIDE) for core in range(2)]


def other_core():
    return [(c, c ^ 1) for c in range(COLS)]


def home_of(y, x, z, core):
    turn = (x - 2 * core) % SIDE
    return (turn + 1) % SIDE // 2, (z + 2 - (y - z)) % SIDE * 2 + turn // 2


def home_to_block():
    pairs = []
    for y in range(SIDE):
        for x in range(SIDE):
            for col in range(COLS):
                half, home = home_of(y, x, col // 2, col % 2)
                pairs.append(((2 * col + half) * COLS + home, (y * SIDE + x) * COLS + col))
    return pairs


def params(limit=12):
    return pltpu.CompilerParams(vmem_limit_bytes=limit * 1024 * 1024)


def whole(count):
    return [pl.BlockSpec(memory_space=pltpu.VMEM)] * count


SCALAR = pl.BlockSpec(memory_space=pltpu.SMEM)
HBM = pl.BlockSpec(memory_space=pltpu.HBM)


def array(shape, dtype):
    return jax.ShapeDtypeStruct(shape, dtype)


def rows_at(start, size):
    return pl.ds(pl.multiple_of(start, 16), size)


def copier(sems):
    count = iter(range(sems.shape[0]))

    def start(source, target):
        copy = pltpu.make_async_copy(source, target, sems.at[next(count)])
        copy.start()
        return copy

    return start


GROUP = 4
CHUNK = 32


def forward_kernel(first, at_ref, *refs):
    tokens_hbm, bias_hbm, q_hbm, wk_hbm, wv_hbm, mask_hbm, row_hbm, dh_hbm, expo_ref, kv_ref, num_ref, stats_ref = refs[:12]
    tokens, w_ref, q_ref, mask_ref, row_ref, dh_ref, bias_ref, tops, score_ref, sems = refs[12:]
    start = copier(sems)
    width, rows = q_ref.shape
    early = [start(wk_hbm, w_ref.at[0]), start(wv_hbm, w_ref.at[1])]
    for n in range(ROWS):
        early.append(start(tokens_hbm.at[n], tokens.at[rows_at(at_ref[first + n], tokens_hbm.shape[1])]))
    late = [start(a, b) for a, b in ((q_hbm, q_ref), (mask_hbm, mask_ref), (row_hbm, row_ref), (dh_hbm, dh_ref))]
    bias_in = [start(bias_hbm.at[h], bias_ref.at[h]) for h in range(HEADS)]
    for copy in early:
        copy.wait()
    for part in range(4):
        span = slice(part * width // 2, (part + 1) * width // 2)
        columns = slice(part % 2 * width // 2, (part % 2 + 1) * width // 2)
        kv_ref[span, :] = dot(w_ref[part // 2, :, columns], tokens[...], ((0,), (1,))).astype(BF16)
    tops[...] = jnp.zeros_like(tops)
    for copy in late:
        copy.wait()
    ones_k = jnp.ones((EXTRA, tokens.shape[0]), BF16)
    ones_q = jnp.ones((EXTRA, rows), BF16)
    live, dead = mask_ref[:HD, :], mask_ref[HD:, :]

    def scores_of(h):
        mine = slice(h * HD, (h + 1) * HD)
        keys = jnp.concatenate([kv_ref[mine, :] * live, dead], axis=0)
        query = jnp.concatenate([q_ref[mine, :], ones_q], axis=0)
        score_ref[h % 2] = tn(query, keys)

    def soften(h):
        lane = lax.broadcasted_iota(jnp.int32, (CHUNK, 128), 1)
        for c in range(0, rows, CHUNK):
            part = slice(c, c + CHUNK)
            scores = score_ref[h % 2, part, :] + bias_ref[h, part, :].astype(F32) * row_ref[0:1, :]
            top = jnp.max(scores, axis=-1, keepdims=True)
            expo_ref[h, part, :] = jnp.exp2(scores - top).astype(BF16)
            tops[part, :] = jnp.where(lane == h, top, tops[part, :])

    def weigh(h):
        mine = slice(h * HD, (h + 1) * HD)
        values = jnp.concatenate([kv_ref[width + h * HD : width + (h + 1) * HD, :], ones_k], axis=0)
        sums = nt(values, expo_ref[h])
        num = sums[:HD]
        num_ref[mine, :] = num
        stats_ref[h : h + 1, :] = sums[HD : HD + 1]
        stats_ref[2 * HEADS + h : 2 * HEADS + h + 1, :] = jnp.sum(num * dh_ref[mine, :].astype(F32), axis=0, keepdims=True)

    scores_of(0)
    for h in range(HEADS):
        if h % GROUP == 0:
            for n in range(h, h + GROUP):
                bias_in[n].wait()
        if h + 1 < HEADS:
            scores_of(h + 1)
        if h:
            weigh(h - 1)
        soften(h)
    weigh(HEADS - 1)

    stats_ref[HEADS : 2 * HEADS, :] = tops[...].T[:HEADS, :]


def forward(at, first, tokens, bias, q, wk, wv, mask, row, dh):
    rows, span = bias.shape[1:]
    width = wk.shape[0]
    return pl.pallas_call(
        functools.partial(forward_kernel, first),
        out_shape=(
            pltpu.VMEM(bias.shape, BF16),
            pltpu.VMEM((2 * width, span), BF16),
            pltpu.VMEM((width, rows), F32),
            array((3 * HEADS, rows), F32),
        ),
        in_specs=[SCALAR] + [HBM] * 8,
        out_specs=tuple(whole(4)),
        scratch_shapes=[
            pltpu.VMEM((span, width), BF16),
            pltpu.VMEM((2, *wk.shape), BF16),
            pltpu.VMEM(q.shape, BF16),
            pltpu.VMEM(mask.shape, BF16),
            pltpu.VMEM(row.shape, F32),
            pltpu.VMEM(dh.shape, BF16),
            pltpu.VMEM(bias.shape, BF16),
            pltpu.VMEM((rows, 128), F32),
            pltpu.VMEM((2, rows, span), F32),
            pltpu.SemaphoreType.DMA((64,)),
        ],
        compiler_params=params(42),
        cost_estimate=pl.CostEstimate(flops=4 * HEADS * rows * span * 256, bytes_accessed=4 * HEADS * rows * span, transcendentals=HEADS * rows * span),
    )(at, tokens, bias, q, wk, wv, mask, row, dh)


def merge(stats):
    top = functools.reduce(jnp.maximum, [s[HEADS : 2 * HEADS, :] for s in stats])
    total, inner = jnp.zeros_like(top), jnp.zeros_like(top)
    for s in stats:
        weight = jnp.exp2(s[HEADS : 2 * HEADS, :] - top)
        total += weight * s[:HEADS, :]
        inner += weight * s[2 * HEADS :, :]
    return total, top, inner


def merge_kernel(left_ref, right_ref, out_ref):
    for n, part in enumerate(merge([left_ref[...], right_ref[...]])):
        out_ref[n * HEADS : (n + 1) * HEADS, :] = part


def merge_pair(left, right):
    return pl.pallas_call(
        merge_kernel,
        out_shape=array(left.shape, F32),
        in_specs=whole(2),
        out_specs=whole(1)[0],
        compiler_params=params(),
    )(left, right)


def backward_kernel(first, at_ref, *refs):
    stats, refs = refs[: SIDE + 1], refs[SIDE + 1 :]
    num_ref, dh_hbm, expo_ref, q_hbm, kv_ref, wk_hbm, wv_hbm, dbias_hbm, dq_hbm, sent_hbm, out_hbm = refs[:11]
    dh_ref, out_ref, dhf_ref, q_ref, w_ref, dbias_ref, dq_ref, dkv, prod_ref, sums, sems = refs[11:]
    start = copier(sems)
    width = q_ref.shape[0]
    early = [start(a, b) for a, b in ((dh_hbm, dh_ref), (q_hbm, q_ref))]
    late = [start(wk_hbm, w_ref.at[0]), start(wv_hbm, w_ref.at[1])]
    total, top, inner = merge([s[...] for s in stats[1:]])
    factor = jnp.exp2(stats[0][HEADS : 2 * HEADS, :] - top) / total
    shift = -factor * (inner / total)
    row = lax.broadcasted_iota(jnp.int32, (EXTRA, shift.shape[1]), 0)
    for copy in early:
        copy.wait()
    ones_k = jnp.ones((EXTRA, kv_ref.shape[1]), BF16)

    def combine(h):
        mine, scale = slice(h * HD, (h + 1) * HD), factor[h : h + 1, :]
        dhf_ref[h * SLOT : h * SLOT + HD, :] = (dh_ref[mine, :].astype(F32) * scale).astype(BF16)
        out_ref[mine, :] = num_ref[mine, :] * scale
        rest, rows = shift[h : h + 1, :], 0.0
        for n in range(3):
            part = rest.astype(BF16).astype(F32)
            rest = rest - part
            rows = jnp.where(row == n, part, rows)
        dhf_ref[h * SLOT + HD : (h + 1) * SLOT, :] = rows.astype(BF16)

    def products(h):
        values = jnp.concatenate([kv_ref[width + h * HD : width + (h + 1) * HD, :], ones_k], axis=0)
        prod_ref[h % 2] = tn(dhf_ref[h * SLOT : (h + 1) * SLOT, :], values)

    def scores(h):
        for c in range(0, prod_ref.shape[1], CHUNK):
            part = slice(c, c + CHUNK)
            dbias_ref[h, part, :] = (expo_ref[h, part, :].astype(F32) * prod_ref[h % 2, part, :]).astype(BF16)

    def to_values(h):
        other = slice(width + h * HD, width + (h + 1) * HD)
        dkv[other, :] = nn(dhf_ref[h * SLOT : h * SLOT + HD, :], expo_ref[h]).astype(BF16)

    def to_queries_and_keys(h):
        mine, d_score = slice(h * HD, (h + 1) * HD), dbias_ref[h]
        dq_ref[mine, :] = (nt(kv_ref[mine, :], d_score) * (1.0 / math.sqrt(HD))).astype(BF16)
        dkv[mine, :] = (nn(q_ref[mine, :], d_score) * LN2).astype(BF16)

    out = []
    combine(0)
    products(0)
    for h in range(HEADS):
        if h + 1 < HEADS:
            combine(h + 1)
            products(h + 1)
        to_values(h)
        if h:
            to_queries_and_keys(h - 1)
        scores(h)
        if h % GROUP == GROUP - 1:
            group = pl.ds(h + 1 - GROUP, GROUP)
            out.append(start(dbias_ref.at[group], dbias_hbm.at[group]))
    to_queries_and_keys(HEADS - 1)
    out.append(start(dq_ref, dq_hbm))
    out.append(start(out_ref, out_hbm))
    for copy in late:
        copy.wait()
    to_tokens = dot(dkv[:width, :], w_ref[0], ((0,), (1,))) + dot(dkv[width:, :], w_ref[1], ((0,), (1,)))
    sums[...] = to_tokens.astype(BF16)
    size = sums.shape[0] // ROWS
    for n in range(ROWS):
        out.append(start(sums.at[rows_at(at_ref[first + n], size)], sent_hbm.at[n]))
    for copy in out:
        copy.wait()


def backward(at, first, own, every, num, dh, expo, q, kv, wk, wv):
    rows, span = expo.shape[1:]
    width = q.shape[0]
    return pl.pallas_call(
        functools.partial(backward_kernel, first),
        out_shape=[array(expo.shape, BF16), array(q.shape, BF16), array((ROWS, span // ROWS, width), BF16), array(num.shape, F32)],
        in_specs=[SCALAR] + whole(SIDE + 2) + [HBM] + whole(1) + [HBM] + whole(1) + [HBM] * 2,
        out_specs=[HBM] * 4,
        scratch_shapes=[
            pltpu.VMEM(dh.shape, BF16),
            pltpu.VMEM(num.shape, F32),
            pltpu.VMEM((HEADS * SLOT, rows), BF16),
            pltpu.VMEM(q.shape, BF16),
            pltpu.VMEM((2, *wk.shape), BF16),
            pltpu.VMEM(expo.shape, BF16),
            pltpu.VMEM(q.shape, BF16),
            pltpu.VMEM((2 * width, span), BF16),
            pltpu.VMEM((2, rows, span), F32),
            pltpu.VMEM((span, width), BF16),
            pltpu.SemaphoreType.DMA((64,)),
        ],
        compiler_params=params(42),
        cost_estimate=pl.CostEstimate(flops=8 * HEADS * rows * span * 256, bytes_accessed=4 * HEADS * rows * span, transcendentals=0),
    )(at, own, *every, num, dh, expo, q, kv, wk, wv)


def prepare_kernel(single_ref, cot_ref, own_ref, own_cot_ref, wq_ref, wg_ref, wo_ref, q_ref, dh_ref, gate_ref, dhid_ref):
    single = single_ref[...]
    q_ref[...] = (dot(wq_ref[...], single, ((0,), (1,))) * (LOG2E / math.sqrt(HD))).astype(BF16)
    gate = jax.nn.sigmoid(dot(wg_ref[...], single, ((0,), (1,))))
    dh_ref[...] = (nt(wo_ref[...], cot_ref[...]) * gate).astype(BF16)
    gate_ref[...] = jax.nn.sigmoid(nn(own_ref[...], wg_ref[...]))
    dhid_ref[...] = nt(own_cot_ref[...], wo_ref[...])


def prepare(single, cotangent, own, wq, wg, wo):
    rows, width = single.shape
    return pl.pallas_call(
        prepare_kernel,
        out_shape=[array((width, rows), BF16)] * 2 + [array(own[0].shape, F32)] * 2,
        in_specs=whole(7),
        out_specs=whole(4),
        compiler_params=params(),
    )(single, cotangent, *own, wq, wg, wo)


def finish_kernel(*refs):
    parts, (gate_ref, dhid_ref, wo_ref, wg_ref, att_ref, rest_ref) = refs[:SIDE], refs[SIDE:]
    size = gate_ref.shape[0]
    both = functools.reduce(jnp.add, [p[...].astype(F32) for p in parts])
    d_query, out, gate = both[:size], both[size:], gate_ref[...]
    att_ref[...] = nn((out * gate).astype(BF16), wo_ref[...]).astype(BF16)
    d_gate = (dhid_ref[...] * out * gate * (1.0 - gate)).astype(BF16)
    rest_ref[...] = d_query + nt(d_gate, wg_ref[...])


def finish(parts, gate, d_hidden, wo, wg):
    return pl.pallas_call(
        finish_kernel,
        out_shape=[array(gate.shape, BF16), array(gate.shape, F32)],
        in_specs=whole(SIDE + 4),
        out_specs=whole(2),
        compiler_params=params(),
    )(*parts, gate, d_hidden, wo, wg)


def query_kernel(first, at_ref, dq_ref, out_ref, w_ref, mine_ref, other_ref, total, turned):
    total[...] = dot(dq_ref[...], w_ref[...], ((0,), (1,)))
    turned[...] = out_ref[...].T
    size = total.shape[0] // COLS
    for n, out in enumerate((mine_ref, other_ref)):
        for k in range(SIDE):
            rows = rows_at(at_ref[first + n * SIDE + k], size)
            out[2 * k * size : (2 * k + 1) * size, :] = total[rows, :].astype(BF16)
            out[(2 * k + 1) * size : (2 * k + 2) * size, :] = turned[rows, :].astype(BF16)


def query(at, first, dq, out, w):
    width, rows = dq.shape
    return pl.pallas_call(
        functools.partial(query_kernel, first),
        out_shape=[array((rows, width), BF16)] * 2,
        in_specs=[SCALAR] + whole(3),
        out_specs=whole(2),
        scratch_shapes=[pltpu.VMEM((rows, width), F32)] * 2,
        compiler_params=params(),
    )(at, dq, out, w)


def split_kernel(left_ref, right_ref, *outs):
    size = outs[0].shape[0]
    for n, out in enumerate(outs):
        rows = slice(n * size, (n + 1) * size)
        out[...] = (left_ref[rows, :].astype(F32) + right_ref[rows, :].astype(F32)).astype(BF16)


def add_split(terms):
    rows, width = terms[0].shape
    return pl.pallas_call(
        split_kernel,
        out_shape=[array((rows // SIDE, width), BF16)] * SIDE,
        in_specs=whole(2),
        out_specs=whole(SIDE),
        compiler_params=params(),
    )(*terms)


def total_kernel(kv_ref, rest_ref, out_ref):
    out_ref[...] = (kv_ref[...].astype(F32) + rest_ref[...]).astype(BF16)


def total(from_kv, rest):
    return pl.pallas_call(
        total_kernel,
        out_shape=array(from_kv.shape, BF16),
        in_specs=whole(2),
        out_specs=whole(1)[0],
        compiler_params=params(),
    )(from_kv, rest)


def join_kernel(first, at_ref, *refs):
    ends, out = refs[:-1], refs[-1]
    size = ends[0].shape[0]
    core = at_ref[first + SIDE]
    for k, end in enumerate(ends):
        shift = core if k < SIDE else size - core
        out[rows_at(at_ref[first + k % SIDE] + shift, size), :] = end[...]


def gather_col(at, first, end):
    near = [end] + [lax.ppermute(end, "col", along_z(k)) for k in (1, 2, 3)]
    far = [lax.ppermute(end, "col", other_core()) for end in near]
    size, width = end.shape
    return pl.pallas_call(
        functools.partial(join_kernel, first),
        out_shape=array((size * COLS, width), BF16),
        in_specs=[SCALAR] + whole(COLS),
        out_specs=whole(1)[0],
        compiler_params=params(),
    )(at, *near, *far)


def shards(single, pair_bias, key_live, w_query, w_key, w_value, w_gate, w_out, cotangent):
    rows, width = single.shape
    span = pair_bias.shape[2]
    piece = rows // COLS
    col_index = lax.axis_index("col")
    z, core = col_index // 2, col_index % 2
    steps = jnp.arange(SIDE, dtype=jnp.int32)
    at = jnp.concatenate([
        ((z + steps) % SIDE * 2 + core) * piece,
        ((z + steps) % SIDE * 2 + 1 - core) * piece,
        (z - steps) % SIDE * 2 * piece,
        core[None] * piece,
        jnp.stack([half * rows + home * piece for y in range(SIDE) for x in range(SIDE) for half, home in [home_of(y, x, z, core)]]),
    ]).astype(jnp.int32)
    both = ("row", "col")

    own = [lax.dynamic_slice_in_dim(a, col_index * piece, piece, 0) for a in (single, cotangent)]
    tokens = lax.ppermute(own[0], both, home_to_block())
    tokens = lax.all_to_all(jnp.broadcast_to(tokens[None], (ROWS, *tokens.shape)), "row", 0, 0)
    q, dh, gate, d_hidden = prepare(single, cotangent, own, w_query, w_gate, w_out)
    alive = key_live[None, :] > 0
    row = jnp.broadcast_to(jnp.where(alive, LOG2E, 0.0).astype(F32), (8, span))
    live = jnp.broadcast_to(alive, (HD, span)).astype(BF16)
    rest, spot = jnp.float32(-30000.0 * LOG2E), lax.broadcasted_iota(jnp.int32, (EXTRA, 1), 0)
    fill = jnp.zeros((EXTRA, 1), F32)
    for n in range(3):
        part = rest.astype(BF16).astype(F32)
        rest = rest - part
        fill = jnp.where(spot == n, part, fill)
    dead = jnp.where(alive, 0.0, fill).astype(BF16)

    mask = jnp.concatenate([live, dead], axis=0)
    expo, kv, num, stats = forward(at, 13, tokens, pair_bias, q, w_key, w_value, mask, row, dh)
    expo, kv, num = (pltpu.with_memory_space_constraint(a, pltpu.VMEM) for a in (expo, kv, num))
    chip = merge_pair(stats, lax.ppermute(stats, "col", other_core()))
    every = [chip] + [lax.ppermute(chip, "col", along_z(k)) for k in (1, 3, 2)]
    d_bias, dq, from_kv, out = backward(at, 13, stats, every, num, dh, expo, q, kv, w_key, w_value)

    from_kv = lax.all_to_all(from_kv, "row", 0, 0)
    mine, other = query(at, 0, dq, out, w_query)
    other = lax.ppermute(other, "col", other_core())
    parts = add_split([mine, other])
    parts = [parts[0]] + [lax.ppermute(parts[k], "col", along_z(k)) for k in (1, 3, 2)]
    attended, rest = finish(parts, gate, d_hidden, w_out, w_gate)
    attended = gather_col(at, 8, attended)
    from_kv = jnp.sum(from_kv.astype(F32), axis=0).astype(BF16)
    from_kv = lax.ppermute(from_kv, both, [(b, a) for a, b in home_to_block()])
    d_single = gather_col(at, 8, total(from_kv, rest))
    return (attended, d_bias, d_single)


def solution(mesh):
    placed = (
        P("row", None),
        P(None, "row", "col"),
        P("col"),
        P(),
        P(),
        P(),
        P(),
        P(),
        P("row", None),
    )
    return jax.shard_map(
        shards,
        mesh=mesh,
        in_specs=placed,
        out_specs=(P("row", None), P(None, "row", "col"), P("row", None)),
        check_vma=False,
    )
```

```python
import functools
import math

import jax
import jax.numpy as jnp
from jax import lax
from jax.experimental import pallas as pl
from jax.experimental.pallas import tpu as pltpu
from jax.sharding import PartitionSpec as P

HEADS = 16
HD = 48
EXTRA = 16
SLOT = HD + EXTRA
LOG2E = math.log2(math.e)
LN2 = math.log(2.0)
ROWS, COLS, SIDE = 16, 8, 4
F32, BF16 = jnp.float32, jnp.bfloat16


def dot(left, right, dims):
    return lax.dot_general(left, right, (dims, ((), ())), preferred_element_type=F32)


def nn(left, right):
    return dot(left, right, ((1,), (0,)))


def nt(left, right):
    return dot(left, right, ((1,), (1,)))


def tn(left, right):
    return dot(left, right, ((0,), (0,)))


def along_z(k):
    return [(z * 2 + core, (z + k) % SIDE * 2 + core) for z in range(SIDE) for core in range(2)]


def other_core():
    return [(c, c ^ 1) for c in range(COLS)]


def home_of(y, x, z, core):
    turn = (x - 2 * core) % SIDE
    return (turn + 1) % SIDE // 2, (z + 2 - (y - z)) % SIDE * 2 + turn // 2


def home_to_block():
    pairs = []
    for y in range(SIDE):
        for x in range(SIDE):
            for col in range(COLS):
                half, home = home_of(y, x, col // 2, col % 2)
                pairs.append(((2 * col + half) * COLS + home, (y * SIDE + x) * COLS + col))
    return pairs


def params(limit=12):
    return pltpu.CompilerParams(vmem_limit_bytes=limit * 1024 * 1024)


def whole(count):
    return [pl.BlockSpec(memory_space=pltpu.VMEM)] * count


SCALAR = pl.BlockSpec(memory_space=pltpu.SMEM)
HBM = pl.BlockSpec(memory_space=pltpu.HBM)


def array(shape, dtype):
    return jax.ShapeDtypeStruct(shape, dtype)


def rows_at(start, size):
    return pl.ds(pl.multiple_of(start, 16), size)


def copier(sems):
    count = iter(range(sems.shape[0]))

    def start(source, target):
        copy = pltpu.make_async_copy(source, target, sems.at[next(count)])
        copy.start()
        return copy

    return start


GROUP = 4
CHUNK = 32


def forward_kernel(first, at_ref, *refs):
    tokens_hbm, bias_hbm, q_hbm, wk_hbm, wv_hbm, mask_hbm, dh_hbm, expo_ref, kv_ref, num_ref, stats_ref = refs[:11]
    tokens, w_ref, q_ref, mask_ref, dh_ref, bias_ref, tops, score_ref, sems = refs[11:]
    start = copier(sems)
    width, rows = q_ref.shape
    early = [start(wk_hbm, w_ref.at[0]), start(wv_hbm, w_ref.at[1])]
    for n in range(ROWS):
        early.append(start(tokens_hbm.at[n], tokens.at[rows_at(at_ref[first + n], tokens_hbm.shape[1])]))
    late = [start(a, b) for a, b in ((q_hbm, q_ref), (mask_hbm, mask_ref), (dh_hbm, dh_ref))]
    bias_in = [start(bias_hbm.at[h], bias_ref.at[h]) for h in range(HEADS)]
    for copy in early:
        copy.wait()
    for part in range(4):
        span = slice(part * width // 2, (part + 1) * width // 2)
        columns = slice(part % 2 * width // 2, (part % 2 + 1) * width // 2)
        kv_ref[span, :] = dot(w_ref[part // 2, :, columns], tokens[...], ((0,), (1,))).astype(BF16)
    tops[...] = jnp.zeros_like(tops)
    for copy in late:
        copy.wait()
    ones_k = jnp.ones((EXTRA, tokens.shape[0]), BF16)
    ones_q = jnp.ones((EXTRA, rows), BF16)
    live, dead = mask_ref[:HD, :], mask_ref[HD:, :]
    factor = mask_ref[:EXTRA, :].astype(F32)[0:1, :] * LOG2E

    def scores_of(h):
        mine = slice(h * HD, (h + 1) * HD)
        keys = jnp.concatenate([kv_ref[mine, :] * live, dead], axis=0)
        query = jnp.concatenate([q_ref[mine, :], ones_q], axis=0)
        score_ref[h % 2] = tn(query, keys)

    def soften(h):
        lane = lax.broadcasted_iota(jnp.int32, (CHUNK, 128), 1)
        for c in range(0, rows, CHUNK):
            part = slice(c, c + CHUNK)
            scores = score_ref[h % 2, part, :] + bias_ref[h, part, :].astype(F32) * factor
            top = jnp.max(scores, axis=-1, keepdims=True)
            expo_ref[h, part, :] = jnp.exp2(scores - top).astype(BF16)
            tops[part, :] = jnp.where(lane == h, top, tops[part, :])

    def weigh(h):
        mine = slice(h * HD, (h + 1) * HD)
        values = jnp.concatenate([kv_ref[width + h * HD : width + (h + 1) * HD, :], ones_k], axis=0)
        sums = nt(values, expo_ref[h])
        num = sums[:HD]
        num_ref[mine, :] = num
        stats_ref[h : h + 1, :] = sums[HD : HD + 1]
        stats_ref[2 * HEADS + h : 2 * HEADS + h + 1, :] = jnp.sum(num * dh_ref[mine, :].astype(F32), axis=0, keepdims=True)

    scores_of(0)
    for h in range(HEADS):
        if h % GROUP == 0:
            for n in range(h, h + GROUP):
                bias_in[n].wait()
        if h + 1 < HEADS:
            scores_of(h + 1)
        if h:
            weigh(h - 1)
        soften(h)
    weigh(HEADS - 1)

    stats_ref[HEADS : 2 * HEADS, :] = tops[...].T[:HEADS, :]


def forward(at, first, tokens, bias, q, wk, wv, mask, dh):
    rows, span = bias.shape[1:]
    width = wk.shape[0]
    return pl.pallas_call(
        functools.partial(forward_kernel, first),
        out_shape=(
            pltpu.VMEM(bias.shape, BF16),
            pltpu.VMEM((2 * width, span), BF16),
            pltpu.VMEM((width, rows), F32),
            array((3 * HEADS, rows), F32),
        ),
        in_specs=[SCALAR] + [HBM] * 7,
        out_specs=tuple(whole(4)),
        scratch_shapes=[
            pltpu.VMEM((span, width), BF16),
            pltpu.VMEM((2, *wk.shape), BF16),
            pltpu.VMEM(q.shape, BF16),
            pltpu.VMEM(mask.shape, BF16),
            pltpu.VMEM(dh.shape, BF16),
            pltpu.VMEM(bias.shape, BF16),
            pltpu.VMEM((rows, 128), F32),
            pltpu.VMEM((2, rows, span), F32),
            pltpu.SemaphoreType.DMA((64,)),
        ],
        compiler_params=params(42),
        cost_estimate=pl.CostEstimate(flops=4 * HEADS * rows * span * 256, bytes_accessed=4 * HEADS * rows * span, transcendentals=HEADS * rows * span),
    )(at, tokens, bias, q, wk, wv, mask, dh)


def merge(stats):
    top = functools.reduce(jnp.maximum, [s[HEADS : 2 * HEADS, :] for s in stats])
    total, inner = jnp.zeros_like(top), jnp.zeros_like(top)
    for s in stats:
        weight = jnp.exp2(s[HEADS : 2 * HEADS, :] - top)
        total += weight * s[:HEADS, :]
        inner += weight * s[2 * HEADS :, :]
    return total, top, inner


def merge_kernel(left_ref, right_ref, out_ref):
    for n, part in enumerate(merge([left_ref[...], right_ref[...]])):
        out_ref[n * HEADS : (n + 1) * HEADS, :] = part


def merge_pair(left, right):
    return pl.pallas_call(
        merge_kernel,
        out_shape=array(left.shape, F32),
        in_specs=whole(2),
        out_specs=whole(1)[0],
        compiler_params=params(),
    )(left, right)


def backward_kernel(first, at_ref, *refs):
    stats, refs = refs[: SIDE + 1], refs[SIDE + 1 :]
    num_ref, dh_hbm, expo_ref, q_hbm, kv_ref, wk_hbm, wv_hbm, dbias_hbm, dq_hbm, sent_hbm, out_hbm = refs[:11]
    dh_ref, out_ref, dhf_ref, q_ref, w_ref, dbias_ref, dq_ref, dkv, prod_ref, sums, sems = refs[11:]
    start = copier(sems)
    width = q_ref.shape[0]
    early = [start(a, b) for a, b in ((dh_hbm, dh_ref), (q_hbm, q_ref))]
    late = [start(wk_hbm, w_ref.at[0]), start(wv_hbm, w_ref.at[1])]
    total, top, inner = merge([s[...] for s in stats[1:]])
    factor = jnp.exp2(stats[0][HEADS : 2 * HEADS, :] - top) / total
    shift = -factor * (inner / total)
    row = lax.broadcasted_iota(jnp.int32, (EXTRA, shift.shape[1]), 0)
    for copy in early:
        copy.wait()
    ones_k = jnp.ones((EXTRA, kv_ref.shape[1]), BF16)

    def combine(h):
        mine, scale = slice(h * HD, (h + 1) * HD), factor[h : h + 1, :]
        dhf_ref[h * SLOT : h * SLOT + HD, :] = (dh_ref[mine, :].astype(F32) * scale).astype(BF16)
        out_ref[mine, :] = num_ref[mine, :] * scale
        rest, rows = shift[h : h + 1, :], 0.0
        for n in range(3):
            part = rest.astype(BF16).astype(F32)
            rest = rest - part
            rows = jnp.where(row == n, part, rows)
        dhf_ref[h * SLOT + HD : (h + 1) * SLOT, :] = rows.astype(BF16)

    def products(h):
        values = jnp.concatenate([kv_ref[width + h * HD : width + (h + 1) * HD, :], ones_k], axis=0)
        prod_ref[h % 2] = tn(dhf_ref[h * SLOT : (h + 1) * SLOT, :], values)

    def scores(h):
        for c in range(0, prod_ref.shape[1], CHUNK):
            part = slice(c, c + CHUNK)
            dbias_ref[h, part, :] = (expo_ref[h, part, :].astype(F32) * prod_ref[h % 2, part, :]).astype(BF16)

    def to_values(h):
        other = slice(width + h * HD, width + (h + 1) * HD)
        dkv[other, :] = nn(dhf_ref[h * SLOT : h * SLOT + HD, :], expo_ref[h]).astype(BF16)

    def to_queries_and_keys(h):
        mine, d_score = slice(h * HD, (h + 1) * HD), dbias_ref[h]
        dq_ref[mine, :] = (nt(kv_ref[mine, :], d_score) * (1.0 / math.sqrt(HD))).astype(BF16)
        dkv[mine, :] = (nn(q_ref[mine, :], d_score) * LN2).astype(BF16)

    out = []
    combine(0)
    products(0)
    for h in range(HEADS):
        if h + 1 < HEADS:
            combine(h + 1)
            products(h + 1)
        to_values(h)
        if h:
            to_queries_and_keys(h - 1)
        scores(h)
        if h % GROUP == GROUP - 1:
            group = pl.ds(h + 1 - GROUP, GROUP)
            out.append(start(dbias_ref.at[group], dbias_hbm.at[group]))
    to_queries_and_keys(HEADS - 1)
    out.append(start(dq_ref, dq_hbm))
    out.append(start(out_ref, out_hbm))
    for copy in late:
        copy.wait()
    to_tokens = dot(dkv[:width, :], w_ref[0], ((0,), (1,))) + dot(dkv[width:, :], w_ref[1], ((0,), (1,)))
    sums[...] = to_tokens.astype(BF16)
    size = sums.shape[0] // ROWS
    for n in range(ROWS):
        out.append(start(sums.at[rows_at(at_ref[first + n], size)], sent_hbm.at[n]))
    for copy in out:
        copy.wait()


def backward(at, first, own, every, num, dh, expo, q, kv, wk, wv):
    rows, span = expo.shape[1:]
    width = q.shape[0]
    return pl.pallas_call(
        functools.partial(backward_kernel, first),
        out_shape=[array(expo.shape, BF16), array(q.shape, BF16), array((ROWS, span // ROWS, width), BF16), array(num.shape, F32)],
        in_specs=[SCALAR] + whole(SIDE + 2) + [HBM] + whole(1) + [HBM] + whole(1) + [HBM] * 2,
        out_specs=[HBM] * 4,
        scratch_shapes=[
            pltpu.VMEM(dh.shape, BF16),
            pltpu.VMEM(num.shape, F32),
            pltpu.VMEM((HEADS * SLOT, rows), BF16),
            pltpu.VMEM(q.shape, BF16),
            pltpu.VMEM((2, *wk.shape), BF16),
            pltpu.VMEM(expo.shape, BF16),
            pltpu.VMEM(q.shape, BF16),
            pltpu.VMEM((2 * width, span), BF16),
            pltpu.VMEM((2, rows, span), F32),
            pltpu.VMEM((span, width), BF16),
            pltpu.SemaphoreType.DMA((64,)),
        ],
        compiler_params=params(42),
        cost_estimate=pl.CostEstimate(flops=8 * HEADS * rows * span * 256, bytes_accessed=4 * HEADS * rows * span, transcendentals=0),
    )(at, own, *every, num, dh, expo, q, kv, wk, wv)


def prepare_kernel(single_ref, cot_ref, own_ref, own_cot_ref, wq_ref, wg_ref, wo_ref, q_ref, dh_ref, gate_ref, dhid_ref):
    single = single_ref[...]
    q_ref[...] = (dot(wq_ref[...], single, ((0,), (1,))) * (LOG2E / math.sqrt(HD))).astype(BF16)
    gate = jax.nn.sigmoid(dot(wg_ref[...], single, ((0,), (1,))))
    dh_ref[...] = (nt(wo_ref[...], cot_ref[...]) * gate).astype(BF16)
    gate_ref[...] = jax.nn.sigmoid(nn(own_ref[...], wg_ref[...]))
    dhid_ref[...] = nt(own_cot_ref[...], wo_ref[...])


def prepare(single, cotangent, own, wq, wg, wo):
    rows, width = single.shape
    return pl.pallas_call(
        prepare_kernel,
        out_shape=[array((width, rows), BF16)] * 2 + [array(own[0].shape, F32)] * 2,
        in_specs=whole(7),
        out_specs=whole(4),
        compiler_params=params(),
    )(single, cotangent, *own, wq, wg, wo)


def finish_kernel(*refs):
    parts, (gate_ref, dhid_ref, wo_ref, wg_ref, att_ref, rest_ref) = refs[:SIDE], refs[SIDE:]
    size = gate_ref.shape[0]
    both = functools.reduce(jnp.add, [p[...].astype(F32) for p in parts])
    d_query, out, gate = both[:size], both[size:], gate_ref[...]
    att_ref[...] = nn((out * gate).astype(BF16), wo_ref[...]).astype(BF16)
    d_gate = (dhid_ref[...] * out * gate * (1.0 - gate)).astype(BF16)
    rest_ref[...] = d_query + nt(d_gate, wg_ref[...])


def finish(parts, gate, d_hidden, wo, wg):
    return pl.pallas_call(
        finish_kernel,
        out_shape=[array(gate.shape, BF16), array(gate.shape, F32)],
        in_specs=whole(SIDE + 4),
        out_specs=whole(2),
        compiler_params=params(),
    )(*parts, gate, d_hidden, wo, wg)


def query_kernel(first, at_ref, dq_ref, out_ref, w_ref, mine_ref, other_ref, total, turned):
    total[...] = dot(dq_ref[...], w_ref[...], ((0,), (1,)))
    turned[...] = out_ref[...].T
    size = total.shape[0] // COLS
    for n, out in enumerate((mine_ref, other_ref)):
        for k in range(SIDE):
            rows = rows_at(at_ref[first + n * SIDE + k], size)
            out[2 * k * size : (2 * k + 1) * size, :] = total[rows, :].astype(BF16)
            out[(2 * k + 1) * size : (2 * k + 2) * size, :] = turned[rows, :].astype(BF16)


def query(at, first, dq, out, w):
    width, rows = dq.shape
    return pl.pallas_call(
        functools.partial(query_kernel, first),
        out_shape=[array((rows, width), BF16)] * 2,
        in_specs=[SCALAR] + whole(3),
        out_specs=whole(2),
        scratch_shapes=[pltpu.VMEM((rows, width), F32)] * 2,
        compiler_params=params(),
    )(at, dq, out, w)


def split_kernel(left_ref, right_ref, *outs):
    size = outs[0].shape[0]
    for n, out in enumerate(outs):
        rows = slice(n * size, (n + 1) * size)
        out[...] = (left_ref[rows, :].astype(F32) + right_ref[rows, :].astype(F32)).astype(BF16)


def add_split(terms):
    rows, width = terms[0].shape
    return pl.pallas_call(
        split_kernel,
        out_shape=[array((rows // SIDE, width), BF16)] * SIDE,
        in_specs=whole(2),
        out_specs=whole(SIDE),
        compiler_params=params(),
    )(*terms)


def total_kernel(kv_ref, rest_ref, out_ref):
    out_ref[...] = (kv_ref[...].astype(F32) + rest_ref[...]).astype(BF16)


def total(from_kv, rest):
    return pl.pallas_call(
        total_kernel,
        out_shape=array(from_kv.shape, BF16),
        in_specs=whole(2),
        out_specs=whole(1)[0],
        compiler_params=params(),
    )(from_kv, rest)


def join_kernel(first, at_ref, *refs):
    core = at_ref[first + SIDE]
    for n, out in enumerate(refs[-2:]):
        ends = refs[n * COLS : (n + 1) * COLS]
        size = ends[0].shape[0]
        for k, end in enumerate(ends):
            shift = core if k < SIDE else size - core
            out[rows_at(at_ref[first + k % SIDE] + shift, size), :] = end[...]


def gather_col(end):
    near = [end] + [lax.ppermute(end, "col", along_z(k)) for k in (1, 2, 3)]
    return near + [lax.ppermute(end, "col", other_core()) for end in near]


def join(at, first, left, right):
    size, width = left[0].shape
    return pl.pallas_call(
        functools.partial(join_kernel, first),
        out_shape=[array((size * COLS, width), BF16)] * 2,
        in_specs=[SCALAR] + whole(2 * COLS),
        out_specs=whole(2),
        compiler_params=params(),
    )(at, *left, *right)


def shards(single, pair_bias, key_live, w_query, w_key, w_value, w_gate, w_out, cotangent):
    rows, width = single.shape
    span = pair_bias.shape[2]
    piece = rows // COLS
    col_index = lax.axis_index("col")
    z, core = col_index // 2, col_index % 2
    steps = jnp.arange(SIDE, dtype=jnp.int32)
    at = jnp.concatenate([
        ((z + steps) % SIDE * 2 + core) * piece,
        ((z + steps) % SIDE * 2 + 1 - core) * piece,
        (z - steps) % SIDE * 2 * piece,
        core[None] * piece,
        jnp.stack([half * rows + home * piece for y in range(SIDE) for x in range(SIDE) for half, home in [home_of(y, x, z, core)]]),
    ]).astype(jnp.int32)
    both = ("row", "col")

    own = [lax.dynamic_slice_in_dim(a, col_index * piece, piece, 0) for a in (single, cotangent)]
    tokens = lax.ppermute(own[0], both, home_to_block())
    tokens = lax.all_to_all(jnp.broadcast_to(tokens[None], (ROWS, *tokens.shape)), "row", 0, 0)
    q, dh, gate, d_hidden = prepare(single, cotangent, own, w_query, w_gate, w_out)
    alive = key_live[None, :] > 0
    live = jnp.broadcast_to(alive, (HD, span)).astype(BF16)
    rest, spot = jnp.float32(-30000.0 * LOG2E), lax.broadcasted_iota(jnp.int32, (EXTRA, 1), 0)
    fill = jnp.zeros((EXTRA, 1), F32)
    for n in range(3):
        part = rest.astype(BF16).astype(F32)
        rest = rest - part
        fill = jnp.where(spot == n, part, fill)
    dead = jnp.where(alive, 0.0, fill).astype(BF16)

    mask = jnp.concatenate([live, dead], axis=0)
    expo, kv, num, stats = forward(at, 13, tokens, pair_bias, q, w_key, w_value, mask, dh)
    expo, kv, num = (pltpu.with_memory_space_constraint(a, pltpu.VMEM) for a in (expo, kv, num))
    chip = merge_pair(stats, lax.ppermute(stats, "col", other_core()))
    every = [chip] + [lax.ppermute(chip, "col", along_z(k)) for k in (1, 3, 2)]
    d_bias, dq, from_kv, out = backward(at, 13, stats, every, num, dh, expo, q, kv, w_key, w_value)

    from_kv = lax.all_to_all(from_kv, "row", 0, 0)
    mine, other = query(at, 0, dq, out, w_query)
    other = lax.ppermute(other, "col", other_core())
    parts = add_split([mine, other])
    parts = [parts[0]] + [lax.ppermute(parts[k], "col", along_z(k)) for k in (1, 3, 2)]
    attended, rest = finish(parts, gate, d_hidden, w_out, w_gate)
    attended = gather_col(attended)
    from_kv = jnp.sum(from_kv.astype(F32), axis=0).astype(BF16)
    from_kv = lax.ppermute(from_kv, both, [(b, a) for a, b in home_to_block()])
    d_single = gather_col(total(from_kv, rest))
    attended, d_single = join(at, 8, attended, d_single)
    return (attended, d_bias, d_single)


def solution(mesh):
    placed = (
        P("row", None),
        P(None, "row", "col"),
        P("col"),
        P(),
        P(),
        P(),
        P(),
        P(),
        P("row", None),
    )
    return jax.shard_map(
        shards,
        mesh=mesh,
        in_specs=placed,
        out_specs=(P("row", None), P(None, "row", "col"), P("row", None)),
        check_vma=False,
    )
```

```python
import functools
import math

import jax
import jax.numpy as jnp
from jax import lax
from jax.experimental import pallas as pl
from jax.experimental.pallas import tpu as pltpu
from jax.sharding import PartitionSpec as P

HEADS = 16
HD = 48
EXTRA = 16
SLOT = HD + EXTRA
LOG2E = math.log2(math.e)
LN2 = math.log(2.0)
ROWS, COLS, SIDE = 16, 8, 4
F32, BF16 = jnp.float32, jnp.bfloat16


def dot(left, right, dims):
    return lax.dot_general(left, right, (dims, ((), ())), preferred_element_type=F32)


def nn(left, right):
    return dot(left, right, ((1,), (0,)))


def nt(left, right):
    return dot(left, right, ((1,), (1,)))


def tn(left, right):
    return dot(left, right, ((0,), (0,)))


def along_z(k):
    return [(z * 2 + core, (z + k) % SIDE * 2 + core) for z in range(SIDE) for core in range(2)]


def other_core():
    return [(c, c ^ 1) for c in range(COLS)]


def home_of(y, x, z, core):
    turn = (x - 2 * core) % SIDE
    return (turn + 1) % SIDE // 2, (z + 2 - (y - z)) % SIDE * 2 + turn // 2


def home_to_block():
    pairs = []
    for y in range(SIDE):
        for x in range(SIDE):
            for col in range(COLS):
                half, home = home_of(y, x, col // 2, col % 2)
                pairs.append(((2 * col + half) * COLS + home, (y * SIDE + x) * COLS + col))
    return pairs


def params(limit=12):
    return pltpu.CompilerParams(vmem_limit_bytes=limit * 1024 * 1024)


def whole(count):
    return [pl.BlockSpec(memory_space=pltpu.VMEM)] * count


SCALAR = pl.BlockSpec(memory_space=pltpu.SMEM)
HBM = pl.BlockSpec(memory_space=pltpu.HBM)


def array(shape, dtype):
    return jax.ShapeDtypeStruct(shape, dtype)


def rows_at(start, size):
    return pl.ds(pl.multiple_of(start, 16), size)


def copier(sems):
    count = iter(range(sems.shape[0]))

    def start(source, target):
        copy = pltpu.make_async_copy(source, target, sems.at[next(count)])
        copy.start()
        return copy

    return start


GROUP = 4
CHUNK = 32


def forward_kernel(first, at_ref, *refs):
    tokens_hbm, bias_hbm, q_hbm, wk_hbm, wv_hbm, mask_hbm, dh_hbm, expo_ref, kv_ref, num_ref, stats_ref = refs[:11]
    tokens, w_ref, q_ref, mask_ref, dh_ref, bias_ref, tops, score_ref, sems = refs[11:]
    start = copier(sems)
    width, rows = q_ref.shape
    early = [start(wk_hbm, w_ref.at[0]), start(wv_hbm, w_ref.at[1])]
    for n in range(ROWS):
        early.append(start(tokens_hbm.at[n], tokens.at[rows_at(at_ref[first + n], tokens_hbm.shape[1])]))
    late = [start(a, b) for a, b in ((q_hbm, q_ref), (mask_hbm, mask_ref), (dh_hbm, dh_ref))]
    bias_in = [start(bias_hbm.at[h], bias_ref.at[h]) for h in range(HEADS)]
    for copy in early:
        copy.wait()
    for part in range(4):
        span = slice(part * width // 2, (part + 1) * width // 2)
        columns = slice(part % 2 * width // 2, (part % 2 + 1) * width // 2)
        kv_ref[span, :] = dot(w_ref[part // 2, :, columns], tokens[...], ((0,), (1,))).astype(BF16)
    tops[...] = jnp.zeros_like(tops)
    for copy in late:
        copy.wait()
    ones_k = jnp.ones((EXTRA, tokens.shape[0]), BF16)
    ones_q = jnp.ones((EXTRA, rows), BF16)
    live, dead = mask_ref[:HD, :], mask_ref[HD:, :]
    factor = mask_ref[:EXTRA, :].astype(F32)[0:1, :] * LOG2E

    def scores_of(h):
        mine = slice(h * HD, (h + 1) * HD)
        keys = jnp.concatenate([kv_ref[mine, :] * live, dead], axis=0)
        query = jnp.concatenate([q_ref[mine, :], ones_q], axis=0)
        score_ref[h % 2] = tn(query, keys)

    def soften(h):
        lane = lax.broadcasted_iota(jnp.int32, (CHUNK, 128), 1)
        for c in range(0, rows, CHUNK):
            part = slice(c, c + CHUNK)
            scores = score_ref[h % 2, part, :] + bias_ref[h, part, :].astype(F32) * factor
            top = jnp.max(scores, axis=-1, keepdims=True)
            expo_ref[h, part, :] = jnp.exp2(scores - top).astype(BF16)
            tops[part, :] = jnp.where(lane == h, top, tops[part, :])

    def weigh(h):
        mine = slice(h * HD, (h + 1) * HD)
        values = jnp.concatenate([kv_ref[width + h * HD : width + (h + 1) * HD, :], ones_k], axis=0)
        sums = nt(values, expo_ref[h])
        num = sums[:HD]
        num_ref[mine, :] = num
        stats_ref[h : h + 1, :] = sums[HD : HD + 1]
        stats_ref[2 * HEADS + h : 2 * HEADS + h + 1, :] = jnp.sum(num * dh_ref[mine, :].astype(F32), axis=0, keepdims=True)

    scores_of(0)
    for h in range(HEADS):
        if h % GROUP == 0:
            for n in range(h, h + GROUP):
                bias_in[n].wait()
        if h + 1 < HEADS:
            scores_of(h + 1)
        if h:
            weigh(h - 1)
        soften(h)
    weigh(HEADS - 1)

    stats_ref[HEADS : 2 * HEADS, :] = tops[...].T[:HEADS, :]


def forward(at, first, tokens, bias, q, wk, wv, mask, dh):
    rows, span = bias.shape[1:]
    width = wk.shape[0]
    return pl.pallas_call(
        functools.partial(forward_kernel, first),
        out_shape=(
            pltpu.VMEM(bias.shape, BF16),
            pltpu.VMEM((2 * width, span), BF16),
            pltpu.VMEM((width, rows), F32),
            array((3 * HEADS, rows), F32),
        ),
        in_specs=[SCALAR] + [HBM] * 7,
        out_specs=tuple(whole(4)),
        scratch_shapes=[
            pltpu.VMEM((span, width), BF16),
            pltpu.VMEM((2, *wk.shape), BF16),
            pltpu.VMEM(q.shape, BF16),
            pltpu.VMEM(mask.shape, BF16),
            pltpu.VMEM(dh.shape, BF16),
            pltpu.VMEM(bias.shape, BF16),
            pltpu.VMEM((rows, 128), F32),
            pltpu.VMEM((2, rows, span), F32),
            pltpu.SemaphoreType.DMA((64,)),
        ],
        compiler_params=params(42),
        cost_estimate=pl.CostEstimate(flops=4 * HEADS * rows * span * 256, bytes_accessed=4 * HEADS * rows * span, transcendentals=HEADS * rows * span),
    )(at, tokens, bias, q, wk, wv, mask, dh)


def merge(stats):
    top = functools.reduce(jnp.maximum, [s[HEADS : 2 * HEADS, :] for s in stats])
    total, inner = jnp.zeros_like(top), jnp.zeros_like(top)
    for s in stats:
        weight = jnp.exp2(s[HEADS : 2 * HEADS, :] - top)
        total += weight * s[:HEADS, :]
        inner += weight * s[2 * HEADS :, :]
    return total, top, inner


def merge_kernel(left_ref, right_ref, out_ref):
    for n, part in enumerate(merge([left_ref[...], right_ref[...]])):
        out_ref[n * HEADS : (n + 1) * HEADS, :] = part


def merge_pair(left, right):
    return pl.pallas_call(
        merge_kernel,
        out_shape=array(left.shape, F32),
        in_specs=whole(2),
        out_specs=whole(1)[0],
        compiler_params=params(),
    )(left, right)


def backward_kernel(first, at_ref, *refs):
    stats, refs = refs[: SIDE + 1], refs[SIDE + 1 :]
    num_ref, dh_hbm, expo_ref, q_hbm, kv_ref, wk_hbm, wv_hbm, dbias_hbm, dq_hbm, sent_hbm, out_hbm = refs[:11]
    dh_ref, out_ref, dhf_ref, q_ref, w_ref, dbias_ref, dq_ref, dkv, prod_ref, sums, sems = refs[11:]
    start = copier(sems)
    width = q_ref.shape[0]
    early = [start(a, b) for a, b in ((dh_hbm, dh_ref), (q_hbm, q_ref))]
    late = [start(wk_hbm, w_ref.at[0]), start(wv_hbm, w_ref.at[1])]
    total, top, inner = merge([s[...] for s in stats[1:]])
    factor = jnp.exp2(stats[0][HEADS : 2 * HEADS, :] - top) / total
    shift = -factor * (inner / total)
    row = lax.broadcasted_iota(jnp.int32, (EXTRA, shift.shape[1]), 0)
    for copy in early:
        copy.wait()
    ones_k = jnp.ones((EXTRA, kv_ref.shape[1]), BF16)

    def combine(h):
        mine, scale = slice(h * HD, (h + 1) * HD), factor[h : h + 1, :]
        dhf_ref[h * SLOT : h * SLOT + HD, :] = (dh_ref[mine, :].astype(F32) * scale).astype(BF16)
        out_ref[mine, :] = num_ref[mine, :] * scale
        rest, rows = shift[h : h + 1, :], 0.0
        for n in range(3):
            part = rest.astype(BF16).astype(F32)
            rest = rest - part
            rows = jnp.where(row == n, part, rows)
        dhf_ref[h * SLOT + HD : (h + 1) * SLOT, :] = rows.astype(BF16)

    def products(h):
        values = jnp.concatenate([kv_ref[width + h * HD : width + (h + 1) * HD, :], ones_k], axis=0)
        prod_ref[h % 2] = tn(dhf_ref[h * SLOT : (h + 1) * SLOT, :], values)

    def scores(h):
        for c in range(0, prod_ref.shape[1], CHUNK):
            part = slice(c, c + CHUNK)
            dbias_ref[h, part, :] = (expo_ref[h, part, :].astype(F32) * prod_ref[h % 2, part, :]).astype(BF16)

    def to_values(h):
        other = slice(width + h * HD, width + (h + 1) * HD)
        dkv[other, :] = nn(dhf_ref[h * SLOT : h * SLOT + HD, :], expo_ref[h]).astype(BF16)

    def to_queries_and_keys(h):
        mine, d_score = slice(h * HD, (h + 1) * HD), dbias_ref[h]
        dq_ref[mine, :] = (nt(kv_ref[mine, :], d_score) * (1.0 / math.sqrt(HD))).astype(BF16)
        dkv[mine, :] = (nn(q_ref[mine, :], d_score) * LN2).astype(BF16)

    out = []
    combine(0)
    products(0)
    for h in range(HEADS):
        if h + 1 < HEADS:
            combine(h + 1)
            products(h + 1)
        to_values(h)
        if h:
            to_queries_and_keys(h - 1)
        scores(h)
        if h % GROUP == GROUP - 1:
            group = pl.ds(h + 1 - GROUP, GROUP)
            out.append(start(dbias_ref.at[group], dbias_hbm.at[group]))
    to_queries_and_keys(HEADS - 1)
    out.append(start(dq_ref, dq_hbm))
    out.append(start(out_ref, out_hbm))
    for copy in late:
        copy.wait()
    to_tokens = dot(dkv[:width, :], w_ref[0], ((0,), (1,))) + dot(dkv[width:, :], w_ref[1], ((0,), (1,)))
    sums[...] = to_tokens.astype(BF16)
    size = sums.shape[0] // ROWS
    for n in range(ROWS):
        out.append(start(sums.at[rows_at(at_ref[first + n], size)], sent_hbm.at[n]))
    for copy in out:
        copy.wait()


def backward(at, first, own, every, num, dh, expo, q, kv, wk, wv):
    rows, span = expo.shape[1:]
    width = q.shape[0]
    return pl.pallas_call(
        functools.partial(backward_kernel, first),
        out_shape=[array(expo.shape, BF16), array(q.shape, BF16), array((ROWS, span // ROWS, width), BF16), array(num.shape, F32)],
        in_specs=[SCALAR] + whole(SIDE + 2) + [HBM] + whole(1) + [HBM] + whole(1) + [HBM] * 2,
        out_specs=[HBM] * 4,
        scratch_shapes=[
            pltpu.VMEM(dh.shape, BF16),
            pltpu.VMEM(num.shape, F32),
            pltpu.VMEM((HEADS * SLOT, rows), BF16),
            pltpu.VMEM(q.shape, BF16),
            pltpu.VMEM((2, *wk.shape), BF16),
            pltpu.VMEM(expo.shape, BF16),
            pltpu.VMEM(q.shape, BF16),
            pltpu.VMEM((2 * width, span), BF16),
            pltpu.VMEM((2, rows, span), F32),
            pltpu.VMEM((span, width), BF16),
            pltpu.SemaphoreType.DMA((64,)),
        ],
        compiler_params=params(42),
        cost_estimate=pl.CostEstimate(flops=8 * HEADS * rows * span * 256, bytes_accessed=4 * HEADS * rows * span, transcendentals=0),
    )(at, own, *every, num, dh, expo, q, kv, wk, wv)


def prepare_kernel(single_ref, cot_ref, own_ref, own_cot_ref, wq_ref, wg_ref, wo_ref, q_ref, dh_ref, gate_ref, dhid_ref):
    single = single_ref[...]
    q_ref[...] = (dot(wq_ref[...], single, ((0,), (1,))) * (LOG2E / math.sqrt(HD))).astype(BF16)
    gate = jax.nn.sigmoid(dot(wg_ref[...], single, ((0,), (1,))))
    dh_ref[...] = (nt(wo_ref[...], cot_ref[...]) * gate).astype(BF16)
    gate_ref[...] = jax.nn.sigmoid(nn(own_ref[...], wg_ref[...]))
    dhid_ref[...] = nt(own_cot_ref[...], wo_ref[...])


def prepare(single, cotangent, own, wq, wg, wo):
    rows, width = single.shape
    return pl.pallas_call(
        prepare_kernel,
        out_shape=[array((width, rows), BF16)] * 2 + [array(own[0].shape, F32)] * 2,
        in_specs=whole(7),
        out_specs=whole(4),
        compiler_params=params(),
    )(single, cotangent, *own, wq, wg, wo)


def finish_kernel(*refs):
    parts, (gate_ref, dhid_ref, wo_ref, wg_ref, _, att_ref, rest_ref) = refs[:SIDE], refs[SIDE:]
    size = gate_ref.shape[0]
    both = functools.reduce(jnp.add, [p[...].astype(F32) for p in parts])
    d_query, out, gate = both[:size], both[size:], gate_ref[...]
    att_ref[...] = nn((out * gate).astype(BF16), wo_ref[...]).astype(BF16)
    d_gate = (dhid_ref[...] * out * gate * (1.0 - gate)).astype(BF16)
    rest_ref[...] = d_query + nt(d_gate, wg_ref[...])


def finish(parts, gate, d_hidden, wo, wg, after):
    return pl.pallas_call(
        finish_kernel,
        out_shape=[array(gate.shape, BF16), array(gate.shape, F32)],
        in_specs=whole(SIDE + 4) + [HBM],
        out_specs=whole(2),
        compiler_params=params(),
    )(*parts, gate, d_hidden, wo, wg, after)


def query_kernel(first, at_ref, dq_ref, out_ref, w_ref, mine_ref, other_ref, total, turned):
    total[...] = dot(dq_ref[...], w_ref[...], ((0,), (1,)))
    turned[...] = out_ref[...].T
    size = total.shape[0] // COLS
    for n, out in enumerate((mine_ref, other_ref)):
        for k in range(SIDE):
            rows = rows_at(at_ref[first + n * SIDE + k], size)
            out[2 * k * size : (2 * k + 1) * size, :] = total[rows, :].astype(BF16)
            out[(2 * k + 1) * size : (2 * k + 2) * size, :] = turned[rows, :].astype(BF16)


def query(at, first, dq, out, w):
    width, rows = dq.shape
    return pl.pallas_call(
        functools.partial(query_kernel, first),
        out_shape=[array((rows, width), BF16)] * 2,
        in_specs=[SCALAR] + whole(3),
        out_specs=whole(2),
        scratch_shapes=[pltpu.VMEM((rows, width), F32)] * 2,
        compiler_params=params(),
    )(at, dq, out, w)


def split_kernel(left_ref, right_ref, *outs):
    size = outs[0].shape[0]
    for n, out in enumerate(outs):
        rows = slice(n * size, (n + 1) * size)
        out[...] = (left_ref[rows, :].astype(F32) + right_ref[rows, :].astype(F32)).astype(BF16)


def add_split(terms):
    rows, width = terms[0].shape
    return pl.pallas_call(
        split_kernel,
        out_shape=[array((rows // SIDE, width), BF16)] * SIDE,
        in_specs=whole(2),
        out_specs=whole(SIDE),
        compiler_params=params(),
    )(*terms)


def total_kernel(kv_ref, rest_ref, out_ref):
    out_ref[...] = (kv_ref[...].astype(F32) + rest_ref[...]).astype(BF16)


def total(from_kv, rest):
    return pl.pallas_call(
        total_kernel,
        out_shape=array(from_kv.shape, BF16),
        in_specs=whole(2),
        out_specs=whole(1)[0],
        compiler_params=params(),
    )(from_kv, rest)


def join_kernel(first, at_ref, *refs):
    core = at_ref[first + SIDE]
    for n, out in enumerate(refs[-2:]):
        ends = refs[n * COLS : (n + 1) * COLS]
        size = ends[0].shape[0]
        for k, end in enumerate(ends):
            shift = core if k < SIDE else size - core
            out[rows_at(at_ref[first + k % SIDE] + shift, size), :] = end[...]


def gather_col(end):
    near = [end] + [lax.ppermute(end, "col", along_z(k)) for k in (1, 2, 3)]
    return near + [lax.ppermute(end, "col", other_core()) for end in near]


def join(at, first, left, right):
    size, width = left[0].shape
    return pl.pallas_call(
        functools.partial(join_kernel, first),
        out_shape=[array((size * COLS, width), BF16)] * 2,
        in_specs=[SCALAR] + whole(2 * COLS),
        out_specs=whole(2),
        compiler_params=params(),
    )(at, *left, *right)


def shards(single, pair_bias, key_live, w_query, w_key, w_value, w_gate, w_out, cotangent):
    rows, width = single.shape
    span = pair_bias.shape[2]
    piece = rows // COLS
    col_index = lax.axis_index("col")
    z, core = col_index // 2, col_index % 2
    steps = jnp.arange(SIDE, dtype=jnp.int32)
    at = jnp.concatenate([
        ((z + steps) % SIDE * 2 + core) * piece,
        ((z + steps) % SIDE * 2 + 1 - core) * piece,
        (z - steps) % SIDE * 2 * piece,
        core[None] * piece,
        jnp.stack([half * rows + home * piece for y in range(SIDE) for x in range(SIDE) for half, home in [home_of(y, x, z, core)]]),
    ]).astype(jnp.int32)
    both = ("row", "col")

    own = [lax.dynamic_slice_in_dim(a, col_index * piece, piece, 0) for a in (single, cotangent)]
    tokens = lax.ppermute(own[0], both, home_to_block())
    tokens = lax.all_to_all(jnp.broadcast_to(tokens[None], (ROWS, *tokens.shape)), "row", 0, 0)
    q, dh, gate, d_hidden = prepare(single, cotangent, own, w_query, w_gate, w_out)
    alive = key_live[None, :] > 0
    live = jnp.broadcast_to(alive, (HD, span)).astype(BF16)
    rest, spot = jnp.float32(-30000.0 * LOG2E), lax.broadcasted_iota(jnp.int32, (EXTRA, 1), 0)
    fill = jnp.zeros((EXTRA, 1), F32)
    for n in range(3):
        part = rest.astype(BF16).astype(F32)
        rest = rest - part
        fill = jnp.where(spot == n, part, fill)
    dead = jnp.where(alive, 0.0, fill).astype(BF16)

    mask = jnp.concatenate([live, dead], axis=0)
    expo, kv, num, stats = forward(at, 13, tokens, pair_bias, q, w_key, w_value, mask, dh)
    expo, kv, num = (pltpu.with_memory_space_constraint(a, pltpu.VMEM) for a in (expo, kv, num))
    chip = merge_pair(stats, lax.ppermute(stats, "col", other_core()))
    every = [chip] + [lax.ppermute(chip, "col", along_z(k)) for k in (1, 3, 2)]
    d_bias, dq, from_kv, out = backward(at, 13, stats, every, num, dh, expo, q, kv, w_key, w_value)

    from_kv = lax.all_to_all(from_kv, "row", 0, 0)
    mine, other = query(at, 0, dq, out, w_query)
    other = lax.ppermute(other, "col", other_core())
    parts = add_split([mine, other])
    parts = [parts[0]] + [lax.ppermute(parts[k], "col", along_z(k)) for k in (1, 3, 2)]
    from_kv = jnp.sum(from_kv.astype(F32), axis=0).astype(BF16)
    attended, rest = finish(parts, gate, d_hidden, w_out, w_gate, from_kv)
    attended = gather_col(attended)
    from_kv = lax.ppermute(from_kv, both, [(b, a) for a, b in home_to_block()])
    d_single = gather_col(total(from_kv, rest))
    attended, d_single = join(at, 8, attended, d_single)
    return (attended, d_bias, d_single)


def solution(mesh):
    placed = (
        P("row", None),
        P(None, "row", "col"),
        P("col"),
        P(),
        P(),
        P(),
        P(),
        P(),
        P("row", None),
    )
    return jax.shard_map(
        shards,
        mesh=mesh,
        in_specs=placed,
        out_specs=(P("row", None), P(None, "row", "col"), P("row", None)),
        check_vma=False,
    )
```
